32 devices in a mesh: group: 2 (over y), tm: 4 (over z), space: 2 (over x), layer: 2 (over core).
Axes of the slice: x: 2, y: 2, z: 4, core: 2. Of those that a mesh axis runs over, the one named last changes fastest.
Arguments:
- state_guess: float32 [16, 64, 16, 128], P('tm', ('group', 'layer'), 'space'), parts along dimension 1, may hold values from -2.5 to 2.5
- start_state: float32 [64, 16, 128], P(('group', 'layer'), 'space'), parts along dimension 0, may hold values from -2.5 to 2.5
- reaction: float32 [64, 16, 128], P(('group', 'layer'), 'space'), parts along dimension 0, may hold values from 0.02 to 0.2
- source: float32 [64, 16, 128], P(('group', 'layer'), 'space'), parts along dimension 0, may hold values from -4 to 4
- self_diag: float32 [16, 128], P('space'), may hold values from 1 to 3
- tiles: bfloat16 [16, 7, 128, 128], P('space'), may hold values from -0.125 to 0.125
- neighbors: int32 [16, 4], P('space'), may hold values from 0 to 15, as said below
Outputs:
- new_state: float32 [16, 64, 16, 128], P('tm', ('group', 'layer'), 'space'), parts along dimension 1
The draws below stay inside these ranges and needn't reach their ends.
There are 2 independent parts, one for each index of `group`. The reference program is written for one: setup_inputs(seed, part) draws one part's arguments, and reference() takes and returns one part's arrays. A program takes and returns all parts, laid end to end along the dimension named above; an argument that names none is the same for every part. Nothing has to cross between parts.
Inputs may be any that keep to these rules, and one draw needn't show every extreme that they name: `neighbors`: row e holds the four elements e - 2, e - 1, e + 1 and e + 2 modulo 16, in an order drawn for each row.
All inputs are finite; a program needn't handle non-finite values.
Results may differ from the reference program's by a relative error of at most 0.0063.
Values may be sent and summed in bfloat16 or wider, within the bound.
No kernel may reach another device: no remote copies, remote signals or barrier semaphores. Data moves between devices by JAX's collectives and lax.ppermute only.
A program may use at most 64 MiB of HBM per device.

```python
import math
import jax
import jax.numpy as jnp

NP = 128
NEWTON = 2
SWEEPS = 2
STEPS = 16
LAYERS = 32
ELEMS = 16


def draw_neighbors(key, part):
    key = jax.random.fold_in(key, 11)
    scores = jax.random.randint(key, (ELEMS, 4), 0, 4096) * 4 + jnp.arange(4, dtype=jnp.int32)[None, :]
    order = jnp.argsort(scores, axis=1)
    choices_table = jnp.array([-2, -1, 1, 2], dtype=jnp.int32)
    offsets = choices_table[order]
    rows = jnp.arange(ELEMS, dtype=jnp.int32)[:, None]
    return ((rows + offsets + ELEMS) % ELEMS).astype(jnp.int32)


def steps_of(key, dims, cuts, least, high):
    loudness, own = 1.0, jax.random.fold_in(key, 6)
    for axis_at, parts in cuts:
        steps = jnp.exp(jax.random.uniform(jax.random.fold_in(own, axis_at), (parts,), jnp.float32, least / len(cuts), high / len(cuts)))
        loudness = loudness * jnp.repeat(steps, dims[axis_at] // parts).reshape([-1 if axis == axis_at else 1 for axis in range(len(dims))])
    return loudness


def noise(key, dims, width, reach, shards=(), held_as=jnp.bfloat16):
    loudness = steps_of(key, dims, shards, -0.22, 0.18) if shards else 1.0
    values = jax.random.normal(key, dims, jnp.float32) * width * loudness
    return jnp.minimum(jnp.maximum(values, -reach), reach).astype(held_as)


def setup_inputs(seed: int = 0, part: int = 0) -> dict:
    seeds = jax.random.split(jax.random.key(seed), 8)
    part_keys = jax.random.split(jax.random.fold_in(seeds[7], part), 8)
    return {
        "state_guess": noise(part_keys[0], (STEPS, LAYERS, ELEMS, NP), 0.6, 2.5, ((0, 4), (1, 2), (2, 2)), jnp.float32),
        "start_state": noise(part_keys[1], (LAYERS, ELEMS, NP), 0.6, 2.5, ((0, 2), (1, 2)), jnp.float32),
        "reaction": jnp.clip(jnp.exp(math.log(0.2) - 2.3025851 * jax.random.uniform(part_keys[2], (LAYERS, ELEMS, NP), jnp.float32) ** steps_of(part_keys[2], (LAYERS, ELEMS, NP), ((0, 2), (1, 2)), -0.2, 0.2)), 0.02, 0.2),
        "source": noise(part_keys[3], (LAYERS, ELEMS, NP), 1.0, 4.0, ((0, 2), (1, 2)), jnp.float32),
        "self_diag": jnp.clip(jnp.exp(math.log(3.0) - 1.0986123 * jax.random.uniform(seeds[4], (ELEMS, NP), jnp.float32) ** steps_of(seeds[4], (ELEMS, NP), ((0, 2),), -0.2, 0.2)), 1.0, 3.0),
        "tiles": noise(seeds[5], (ELEMS, 7, NP, NP), (16 * NP) ** -0.5, 0.125, ((0, 2),)),
        "neighbors": draw_neighbors(jax.random.fold_in(seeds[7], 71), part),
    }


corner_weight = 0.25


def transform_tables(steps):
    beta = corner_weight ** (1.0 / steps)
    counter = jnp.arange(steps, dtype=jnp.int32)
    product = (counter[:, None] * counter[None, :]) % steps
    angle = product.astype(jnp.float32) * (2.0 * math.pi / steps)
    times = counter.astype(jnp.float32)
    rising = jnp.power(jnp.float32(beta), times)
    falling = jnp.power(jnp.float32(beta), -times) / steps
    fwd_re = (jnp.cos(angle) * rising[None, :]).astype(jnp.bfloat16)
    fwd_im = (-jnp.sin(angle) * rising[None, :]).astype(jnp.bfloat16)
    back_re = (jnp.cos(angle) * falling[:, None]).astype(jnp.bfloat16)
    back_im = (-jnp.sin(angle) * falling[:, None]).astype(jnp.bfloat16)
    phase = times * (2.0 * math.pi / steps)
    eigen_re = 1.0 - beta * jnp.cos(phase)
    eigen_im = beta * jnp.sin(phase)
    return fwd_re, fwd_im, back_re, back_im, eigen_re, eigen_im


def tile_part(rounded, tiles, neighbors):
    wide = rounded.astype(jnp.float32)
    blocks = tiles.astype(jnp.float32)
    total = jnp.einsum("rlep,epq->rleq", wide, blocks[:, 0])
    for slot in range(4):
        moved = jnp.take(wide, neighbors[:, slot], axis=2)
        total = total + jnp.einsum("rlep,epq->rleq", moved, blocks[:, slot + 1])
    below = jnp.pad(wide, ((0, 0), (1, 0), (0, 0), (0, 0)))[:, :-1]
    above = jnp.pad(wide, ((0, 0), (0, 1), (0, 0), (0, 0)))[:, 1:]
    total = total + jnp.einsum("rlep,epq->rleq", below, blocks[:, 5])
    total = total + jnp.einsum("rlep,epq->rleq", above, blocks[:, 6])
    return total


def divide(num_re, num_im, inverse_re, inverse_im):
    return inverse_re * num_re - inverse_im * num_im, inverse_im * num_re + inverse_re * num_im


def reference(state_guess, start_state, reaction, source, self_diag, tiles, neighbors):
    steps = state_guess.shape[0]
    fwd_re, fwd_im, back_re, back_im, eigen_re, eigen_im = transform_tables(steps)
    jacobian = 3.0 * reaction * start_state * start_state
    diag_re = eigen_re[:, None, None, None] + self_diag[None, None] + jacobian[None]
    square_im = (eigen_im * eigen_im)[:, None, None, None]
    denom = diag_re * diag_re + square_im
    inverse_re = diag_re / denom
    inverse_im = -eigen_im[:, None, None, None] / denom
    state = state_guess
    for newton_step in range(NEWTON):
        rounded = state.astype(jnp.bfloat16)
        image = self_diag * state + tile_part(rounded[:], tiles, neighbors)
        previous = jnp.concatenate([start_state[None], state[:-1]], 0)
        residual = state - previous + image + reaction * state * state * state - source
        rhs = (-residual).astype(jnp.bfloat16).astype(jnp.float32)
        spec_re = jnp.einsum("kt,tlep->klep", fwd_re.astype(jnp.float32), rhs).astype(jnp.bfloat16).astype(jnp.float32)
        spec_im = jnp.einsum("kt,tlep->klep", fwd_im.astype(jnp.float32), rhs).astype(jnp.bfloat16).astype(jnp.float32)
        sol_re, sol_im = divide(spec_re, spec_im, inverse_re, inverse_im)
        for sweep in range(SWEEPS - 1):
            packed = jnp.concatenate([sol_re.astype(jnp.bfloat16), sol_im.astype(jnp.bfloat16)], 0)
            applied = tile_part(packed, tiles, neighbors)
            sol_re, sol_im = divide(spec_re - applied[:steps], spec_im - applied[steps:], inverse_re, inverse_im)
        final_re = sol_re.astype(jnp.bfloat16).astype(jnp.float32)
        final_im = sol_im.astype(jnp.bfloat16).astype(jnp.float32)
        delta = jnp.einsum("tk,klep->tlep", back_re.astype(jnp.float32), final_re)
        delta = delta + jnp.einsum("tk,klep->tlep", back_im.astype(jnp.float32), final_im)
        state = state + delta.astype(jnp.bfloat16).astype(jnp.float32)
    return state
```

```python
import math

import jax
import jax.numpy as jnp
import numpy as np
from jax import lax
from jax.experimental import pallas as pl
from jax.experimental.pallas import tpu as pltpu
from jax.sharding import PartitionSpec as P

NEWTON = 2
APPLICATIONS = 2 * NEWTON
OFFSETS = (-2, -1, 1, 2)
GROUP = 4

corner_weight = 0.25


def transform_tables(steps):
    beta = corner_weight ** (1.0 / steps)
    half = steps // 2
    counter = np.arange(steps)
    angle = ((counter[:, None] * counter[None, :]) % steps) * (2.0 * math.pi / steps)
    rising = np.power(beta, counter)
    falling = np.power(beta, -counter.astype(np.float64)) / steps
    fwd_re = np.cos(angle) * rising[None, :]
    fwd_im = -np.sin(angle) * rising[None, :]
    back_re = np.cos(angle) * falling[:, None]
    back_im = -np.sin(angle) * falling[:, None]
    forward = np.concatenate([fwd_re[:half], fwd_re[half : half + 1], fwd_im[1:half]], 0)
    twice = np.where(np.arange(half) == 0, 1.0, 2.0)
    backward = np.concatenate(
        [
            back_re[:, :half] * twice,
            back_re[:, half : half + 1],
            back_im[:, 1:half] * 2.0,
        ],
        1,
    )
    phase = counter * (2.0 * math.pi / steps)
    eigen_re = 1.0 - beta * np.cos(phase)
    eigen_im = beta * np.sin(phase)
    low_re = eigen_re[:half]
    low_im = np.where(np.arange(half) == 0, 0.0, eigen_im[:half])
    high_re = np.concatenate([eigen_re[half : half + 1], eigen_re[1:half]])
    eigen = np.stack([low_re, low_im, high_re]).astype(np.float32)
    return forward, backward, eigen


def newton(values, old, tiles, slots, coef, diag, eigen, forward, backward, packed, spec, inverse,
           base, window_at, all_layers, write):
    layers, steps, width = values.shape[1:]
    half = steps // 2
    wide, inner = layers - 2, layers - 4

    def applied(array, at, low, count, element):
        parts = [array[at, low : low + count]]
        for offset in OFFSETS:
            parts.append(array[at + offset, low : low + count])
        parts.append(array[at, low - 1 : low - 1 + count])
        parts.append(array[at, low + 1 : low + 1 + count])
        rows = jnp.concatenate([part.reshape(count * steps, width) for part in parts], axis=1)
        blocks = [tiles[element, 0]]
        for place in range(4):
            blocks.append(tiles[element, slots[element, place]])
        blocks.append(tiles[element, 5])
        blocks.append(tiles[element, 6])
        weights = jnp.concatenate(blocks, axis=0)
        out = jnp.dot(rows, weights, preferred_element_type=jnp.float32)
        return out.reshape(count, steps, width)

    layer = lax.broadcasted_iota(jnp.int32, (wide, 1, width), 0) + (base + window_at + 1)
    inside = jnp.where((layer >= 0) & (layer < all_layers), 1.0, 0.0).astype(jnp.float32)
    time = lax.broadcasted_iota(jnp.int32, (wide, steps, width), 1)
    for element in range(8):
        image = applied(values, element + 2, 1, wide, element)
        state = values[element + 2, 1 : 1 + wide].astype(jnp.float32)
        rows = slice(window_at + 1, window_at + 1 + wide)
        start = coef[0, rows, element : element + 1, :]
        reaction = coef[1, rows, element : element + 1, :]
        source = coef[2, rows, element : element + 1, :]
        own = diag[element : element + 1, :][None]
        previous = jnp.where(time == 0, start, pltpu.roll(state, 1, 1))
        residual = (
            state - previous + own * state + image + reaction * state * state * state - source
        )
        rhs = (-residual).astype(jnp.bfloat16).reshape(wide * steps, width)
        out = jnp.dot(forward[...], rhs, preferred_element_type=jnp.float32)
        out = out.astype(jnp.bfloat16).astype(jnp.float32).reshape(wide, steps, width)
        real = own + 3.0 * reaction * start * start
        low = eigen[0][None] + real
        high = eigen[2][None] + real
        imag = eigen[1][None]
        low_over = inside / (low * low + imag * imag)
        high_over = inside / (high * high + imag * imag)
        first = low * low_over
        cross = -imag * low_over
        last = high * high_over
        part_a, part_b = out[:, :half], out[:, half:]
        sol = jnp.concatenate(
            [first * part_a - cross * part_b, cross * part_a + last * part_b], axis=1
        )
        packed[element] = sol.astype(jnp.bfloat16)
        if 2 <= element < 6:
            spec[element - 2] = out
            inverse[element - 2, 0] = first
            inverse[element - 2, 1] = cross
            inverse[element - 2, 2] = last
    for own in range(4):
        image = applied(packed, own + 2, 1, inner, own + 2)
        left = spec[own, 1 : 1 + inner] - image
        part_a, part_b = left[:, :half], left[:, half:]
        first = inverse[own, 0, 1 : 1 + inner]
        cross = inverse[own, 1, 1 : 1 + inner]
        last = inverse[own, 2, 1 : 1 + inner]
        final = jnp.concatenate(
            [first * part_a - cross * part_b, cross * part_a + last * part_b], axis=1
        )
        final = final.astype(jnp.bfloat16).reshape(inner * steps, width)
        delta = jnp.dot(backward[...], final, preferred_element_type=jnp.float32)
        delta = delta.astype(jnp.bfloat16).astype(jnp.float32).reshape(inner, steps, width)
        state = values[own + 4, 2 : 2 + inner].astype(jnp.float32) + delta
        write(own, state.astype(jnp.bfloat16))


def first_kernel(all_layers, where, slots, own, beside, across, order, tiles, coef, diag, eigen,
                 forward, backward, out, values, packed, spec, inverse):
    steps, rows, width = own.shape
    core = where[0]
    size = steps * GROUP * 4
    for group in range(rows // (GROUP * 4)):
        cut = pl.ds(group * GROUP * 4, GROUP * 4)
        near, far = beside[:, cut, :], across[:, cut, :]
        left = jnp.where(core == 0, far, near)
        right = jnp.where(core == 0, near, far)
        for at, part in ((0, left), (4, own[:, cut, :]), (8, right)):
            moved = jnp.dot(
                order[...], part.reshape(size, width), preferred_element_type=jnp.float32
            )
            moved = moved.astype(jnp.bfloat16).reshape(4, GROUP, steps, width)
            values[at : at + 4, group * GROUP : (group + 1) * GROUP] = moved

    def write(element, state):
        out[element] = state

    newton(values, None, tiles, slots, coef, diag, eigen, forward, backward, packed, spec, inverse,
           where[1], 0, all_layers, write)


def second_kernel(all_layers, where, slots, own, beside, across, order, tiles, coef, diag, eigen,
                  forward, backward, out, values, packed, spec, inverse, solved):
    core = where[0]
    near, far = beside[...], across[...]
    values[0:4] = jnp.where(core == 0, far, near)
    values[4:8] = own[...]
    values[8:12] = jnp.where(core == 0, near, far)
    steps, width = own.shape[2:]

    def write(element, state):
        solved[element] = state

    newton(values, None, tiles, slots, coef, diag, eigen, forward, backward, packed, spec, inverse,
           where[1], 2, all_layers, write)
    size = steps * GROUP * 4
    for group in range(solved.shape[1] // GROUP):
        part = solved[:, group * GROUP : (group + 1) * GROUP].reshape(size, width)
        moved = jnp.dot(order[...], part, preferred_element_type=jnp.float32)
        cut = pl.ds(group * GROUP * 4, GROUP * 4)
        out[:, cut, :] = moved.astype(jnp.bfloat16).reshape(steps, GROUP * 4, width)


def call(kernel, out_shape, scratch, scalars, arrays):
    return pl.pallas_call(
        kernel,
        out_shape=jax.ShapeDtypeStruct(out_shape, jnp.bfloat16),
        in_specs=[pl.BlockSpec(memory_space=pltpu.SMEM)] * len(scalars)
        + [pl.BlockSpec(memory_space=pltpu.VMEM)] * len(arrays),
        out_specs=pl.BlockSpec(memory_space=pltpu.VMEM),
        scratch_shapes=scratch,
        compiler_params=pltpu.CompilerParams(vmem_limit_bytes=48 * 1024 * 1024),
    )(*scalars, *arrays)


def shards(state_guess, start_state, reaction, source, self_diag, tiles, neighbors):
    local_steps, local_layers, local_elems, width = state_guess.shape
    count = lax.axis_size("tm")
    sections = lax.axis_size("space")
    mine, core = lax.axis_index("tm"), lax.axis_index("layer")
    steps = local_steps * count
    all_layers = local_layers * 2
    chip_layers = all_layers // count
    window = -(-(chip_layers + 2 * APPLICATIONS) // GROUP) * GROUP
    half = local_elems // 2
    swap = [(0, 1), (1, 0)]
    circle = []
    for section in range(sections):
        one, other = 2 * section + 1, 2 * ((section + 1) % sections)
        circle += [(one, other), (other, one)]

    def over_core(array):
        return lax.ppermute(array, "layer", swap)

    def over_circle(array):
        return lax.ppermute(array, ("space", "layer"), circle)

    def exchanged(parts):
        return [parts[0]] + [
            lax.ppermute(parts[k], "tm", [(i, i ^ k) for i in range(count)])
            for k in range(1, count)
        ]

    forward, backward, eigen = transform_tables(steps)
    low = lax.bitwise_xor(mine, jnp.arange(count, dtype=jnp.int32)) * local_steps
    times = (low[:, None] + jnp.arange(local_steps, dtype=jnp.int32)[None]).reshape(steps)
    size = 4 * GROUP * steps
    row = jnp.arange(size, dtype=jnp.int32)
    solver = (row // (GROUP * steps), row // steps % GROUP, row % steps)
    arrival = (row % 4, row // 4 % GROUP, jnp.repeat(times, GROUP * 4))
    target = (solver[0] * GROUP + solver[1]) * steps + solver[2]
    from_there = (arrival[0] * GROUP + arrival[1]) * steps + arrival[2]
    order = (target[:, None] == from_there[None, :]).astype(jnp.bfloat16)
    order_back = (from_there[:, None] == target[None, :]).astype(jnp.bfloat16)

    pair = state_guess.astype(jnp.bfloat16).reshape(local_steps, local_layers, 2, half, width)
    flat = (local_steps, local_layers * half, width)
    keep = lax.dynamic_index_in_dim(pair, core, 2, keepdims=False).reshape(flat)
    give = lax.dynamic_index_in_dim(pair, 1 - core, 2, keepdims=False).reshape(flat)
    got = over_core(give)
    below = jnp.zeros((local_steps, APPLICATIONS * half, width), jnp.bfloat16)
    above = jnp.zeros(
        (local_steps, (window - chip_layers - APPLICATIONS) * half, width), jnp.bfloat16
    )
    whole = jnp.concatenate(
        [below, jnp.where(core == 0, keep, got), jnp.where(core == 0, got, keep), above], 1
    )
    pieces = [
        lax.dynamic_slice_in_dim(
            whole, lax.bitwise_xor(mine, k) * (chip_layers * half), window * half, 1
        )
        for k in range(count)
    ]
    own = jnp.concatenate(exchanged(pieces), 0)

    at = 4 * core
    edge_tiles = lax.dynamic_slice_in_dim(tiles, 6 * core, 2, 0)
    edge_tiles = over_circle(edge_tiles)
    near_tiles = lax.dynamic_slice_in_dim(
        jnp.concatenate([edge_tiles, tiles, edge_tiles], 0), at, 8, 0
    )
    total = local_elems * sections
    ids = lax.axis_index("space") * local_elems + jnp.arange(local_elems, dtype=jnp.int32)
    wanted = (ids[:, None] + jnp.array(OFFSETS, jnp.int32)[None] + total) % total
    slots = jnp.sum(
        (wanted[:, :, None] == neighbors[:, None, :])
        * jnp.arange(1, 5, dtype=jnp.int32)[None, None],
        -1,
    )
    fields = jnp.stack([start_state, reaction, source])
    other = over_core(fields)
    fields = jnp.concatenate(
        [jnp.where(core == 0, fields, other), jnp.where(core == 0, other, fields)], 1
    )
    fields = jnp.pad(
        fields,
        ((0, 0), (APPLICATIONS, window - chip_layers - APPLICATIONS), (0, 0), (0, 0)),
    )
    fields = lax.dynamic_slice_in_dim(fields, mine * chip_layers, window, 1)
    slot_rows = jnp.pad(slots.astype(jnp.float32), ((0, 0), (0, width - 4)))
    bundle = jnp.concatenate(
        [fields.reshape(3 * window, local_elems, width), self_diag[None], slot_rows[None]], 0
    )
    edge = over_circle(lax.dynamic_slice_in_dim(bundle, 6 * core, 2, 1))
    bundle = lax.dynamic_slice_in_dim(jnp.concatenate([edge, bundle, edge], 1), at, 8, 1)
    coef = bundle[: 3 * window].reshape(3, window, 8, width)
    diag = bundle[3 * window]
    slots = bundle[3 * window + 1, :, :4].astype(jnp.int32)
    place = jnp.stack([core, mine * chip_layers - APPLICATIONS]).astype(jnp.int32)
    eigen = jnp.asarray(np.broadcast_to(eigen[:, :, None], eigen.shape + (width,)))

    def table(matrix, layers):
        return jnp.asarray(np.kron(np.eye(layers), matrix).astype(np.float32)).astype(jnp.bfloat16)

    def scratch(layers):
        return [
            pltpu.VMEM((12, layers, steps, width), jnp.bfloat16),
            pltpu.VMEM((8, layers - 2, steps, width), jnp.bfloat16),
            pltpu.VMEM((4, layers - 2, steps, width), jnp.float32),
            pltpu.VMEM((4, 3, layers - 2, steps // 2, width), jnp.float32),
        ]

    state = call(
        lambda *refs: first_kernel(all_layers, *refs),
        (4, window - 4, steps, width),
        scratch(window),
        [place, slots],
        [own, over_core(own), over_circle(own), order, near_tiles, coef, diag, eigen,
         table(forward, window - 2), table(backward, window - 4)],
    )
    last = window - 8
    solved = call(
        lambda *refs: second_kernel(all_layers, *refs),
        (steps, last * half, width),
        scratch(window - 4) + [pltpu.VMEM((4, last, steps, width), jnp.bfloat16)],
        [place, slots],
        [state, over_core(state), over_circle(state), order_back, near_tiles, coef, diag, eigen,
         table(forward, window - 6), table(backward, last)],
    )
    parts = exchanged([solved[k * local_steps : (k + 1) * local_steps] for k in range(count)])
    parts = jnp.stack(parts).reshape(2, count // 2, local_steps, last, half, width)
    parts = parts[:, :, :, :chip_layers]
    same = (mine // (count // 2)) == core
    keep = jnp.where(same, parts[0], parts[1])
    got = over_core(jnp.where(same, parts[1], parts[0]))
    both = jnp.concatenate(
        [jnp.where(core == 0, keep, got), jnp.where(core == 0, got, keep)], 3
    )
    ranks = lax.bitwise_xor(
        mine % (count // 2), jnp.arange(count // 2, dtype=jnp.int32)
    )
    both = jnp.take(both, ranks, axis=0)
    both = jnp.transpose(both, (1, 0, 2, 3, 4))
    return both.reshape(state_guess.shape).astype(jnp.float32)


def solution(mesh):
    in_specs = (
        P("tm", ("group", "layer"), "space", None),
        P(("group", "layer"), "space", None),
        P(("group", "layer"), "space", None),
        P(("group", "layer"), "space", None),
        P("space", None),
        P("space", None, None, None),
        P("space", None),
    )
    out_specs = P("tm", ("group", "layer"), "space", None)
    return jax.shard_map(shards, mesh=mesh, in_specs=in_specs, out_specs=out_specs, check_vma=False)
```

```python
import math

import jax
import jax.numpy as jnp
import numpy as np
from jax import lax
from jax.experimental import pallas as pl
from jax.experimental.pallas import tpu as pltpu
from jax.sharding import PartitionSpec as P

NEWTON = 2
APPLICATIONS = 2 * NEWTON
OFFSETS = (-2, -1, 1, 2)
GROUP = 4

corner_weight = 0.25


def transform_tables(steps):
    beta = corner_weight ** (1.0 / steps)
    half = steps // 2
    counter = np.arange(steps)
    angle = ((counter[:, None] * counter[None, :]) % steps) * (2.0 * math.pi / steps)
    rising = np.power(beta, counter)
    falling = np.power(beta, -counter.astype(np.float64)) / steps
    fwd_re = np.cos(angle) * rising[None, :]
    fwd_im = -np.sin(angle) * rising[None, :]
    back_re = np.cos(angle) * falling[:, None]
    back_im = -np.sin(angle) * falling[:, None]
    forward = np.concatenate([fwd_re[:half], fwd_re[half : half + 1], fwd_im[1:half]], 0)
    twice = np.where(np.arange(half) == 0, 1.0, 2.0)
    backward = np.concatenate(
        [
            back_re[:, :half] * twice,
            back_re[:, half : half + 1],
            back_im[:, 1:half] * 2.0,
        ],
        1,
    )
    phase = counter * (2.0 * math.pi / steps)
    eigen_re = 1.0 - beta * np.cos(phase)
    eigen_im = beta * np.sin(phase)
    low_re = eigen_re[:half]
    low_im = np.where(np.arange(half) == 0, 0.0, eigen_im[:half])
    high_re = np.concatenate([eigen_re[half : half + 1], eigen_re[1:half]])
    eigen = np.stack([low_re, low_im, high_re]).astype(np.float32)
    return forward, backward, eigen


def newton(values, weights_of, coef, diag, forward, backward, packed, spec, inverse,
           base, window_at, all_layers, write):
    layers, steps, width = values.shape[1:]
    half = steps // 2
    wide, inner = layers - 2, layers - 4
    sublane = lax.broadcasted_iota(jnp.int32, (half, width), 0)
    eigen = []
    for numbers in transform_tables(steps)[2]:
        column = jnp.full((half, width), float(numbers[0]), jnp.float32)
        for at in range(1, half):
            column = jnp.where(sublane == at, float(numbers[at]), column)
        eigen.append(column)

    def applied(array, at, low, count, element):
        parts = [array[at, low : low + count]]
        for offset in OFFSETS:
            parts.append(array[at + offset, low : low + count])
        parts.append(array[at, low - 1 : low - 1 + count])
        parts.append(array[at, low + 1 : low + 1 + count])
        rows = jnp.concatenate([part.reshape(count * steps, width) for part in parts], axis=1)
        weights = jnp.concatenate(weights_of(element), axis=0)
        out = jnp.dot(rows, weights, preferred_element_type=jnp.float32)
        return out.reshape(count, steps, width)

    for element in range(8):
        mid = 2 <= element < 6
        low, count = (1, wide) if mid else (2, inner)
        image = applied(values, element + 2, low, count, element)
        state = values[element + 2, low : low + count].astype(jnp.float32)
        rows = slice(window_at + low, window_at + low + count)
        start = coef[0, rows, element : element + 1, :]
        reaction = coef[1, rows, element : element + 1, :]
        source = coef[2, rows, element : element + 1, :]
        own = diag[element : element + 1, :][None]
        time = lax.broadcasted_iota(jnp.int32, (count, steps, width), 1)
        previous = jnp.where(time == 0, start, pltpu.roll(state, 1, 1))
        residual = (
            state - previous + own * state + image + reaction * state * state * state - source
        )
        rhs = (-residual).astype(jnp.bfloat16).reshape(count * steps, width)
        cut = count * steps
        out = jnp.dot(forward[:cut, :cut], rhs, preferred_element_type=jnp.float32)
        out = out.astype(jnp.bfloat16).astype(jnp.float32).reshape(count, steps, width)
        layer = lax.broadcasted_iota(jnp.int32, (count, 1, width), 0) + (base + window_at + low)
        inside = jnp.where((layer >= 0) & (layer < all_layers), 1.0, 0.0).astype(jnp.float32)
        real = own + 3.0 * reaction * start * start
        near = eigen[0][None] + real
        far = eigen[2][None] + real
        imag = eigen[1][None]
        near_over = inside / (near * near + imag * imag)
        far_over = inside / (far * far + imag * imag)
        first = near * near_over
        cross = -imag * near_over
        last = far * far_over
        part_a, part_b = out[:, :half], out[:, half:]
        sol = jnp.concatenate(
            [first * part_a - cross * part_b, cross * part_a + last * part_b], axis=1
        )
        packed[element, low - 1 : low - 1 + count] = sol.astype(jnp.bfloat16)
        if mid:
            spec[element - 2] = out
            inverse[element - 2, 0] = first
            inverse[element - 2, 1] = cross
            inverse[element - 2, 2] = last
    for own in range(4):
        image = applied(packed, own + 2, 1, inner, own + 2)
        left = spec[own, 1 : 1 + inner] - image
        part_a, part_b = left[:, :half], left[:, half:]
        first = inverse[own, 0, 1 : 1 + inner]
        cross = inverse[own, 1, 1 : 1 + inner]
        last = inverse[own, 2, 1 : 1 + inner]
        final = jnp.concatenate(
            [first * part_a - cross * part_b, cross * part_a + last * part_b], axis=1
        )
        final = final.astype(jnp.bfloat16).reshape(inner * steps, width)
        delta = jnp.dot(backward[...], final, preferred_element_type=jnp.float32)
        delta = delta.astype(jnp.bfloat16).astype(jnp.float32).reshape(inner, steps, width)
        state = values[own + 4, 2 : 2 + inner].astype(jnp.float32) + delta
        write(own, state.astype(jnp.bfloat16))


def chooser(where, tiles, edge_tiles, total):
    core, first = where[0, 0], where[0, 2]

    def blocks(table, ids, at, element, row):
        places = [0]
        for offset in OFFSETS:
            wanted = lax.rem(element + (offset + total), total)
            slot = jnp.int32(1)
            for column in range(1, 4):
                slot = jnp.where(where[ids + column, at] == wanted, column + 1, slot)
            places.append(slot)
        return [table[row, place] for place in places + [5, 6]]

    def weights_of(element):
        local = element - 2 + 4 * core
        number = first + local + total
        if 2 <= element < 6:
            return blocks(tiles, 1, local, number, local)
        outer = element if element < 2 else element - 6
        inside = element + 2 if element < 2 else element - 2
        here = blocks(tiles, 1, inside, number, inside)
        there = blocks(edge_tiles, 5, 6 - 6 * core + outer, number, outer)
        away = core == (0 if element < 2 else 1)
        return [jnp.where(away, two, one) for one, two in zip(here, there)]

    return weights_of


def fields_kernel(where, start, reaction, source, start_two, reaction_two, source_two, diag,
                  ids, _, bundle, edge):
    layers = start.shape[0]
    core, base = where[0], where[1]
    window = bundle.shape[0] // 3
    for at, (one, two) in enumerate(
        ((start, start_two), (reaction, reaction_two), (source, source_two))
    ):
        for place in range(window):
            layer = jnp.clip(base + place, 0, 2 * layers - 1)
            own = layer // layers == core
            layer = lax.rem(layer, layers)
            row = jnp.where(own, one[layer], two[layer])
            bundle[at * window + place] = row
            edge[at * window + place] = jnp.where(core == 0, row[0:2], row[6:8])
    edge[3 * window] = jnp.where(core == 0, diag[0:2], diag[6:8])
    for at in range(2):
        edge[3 * window + 1 + at, :, 0:8] = ids[2 * at : 2 * at + 2].astype(jnp.float32)


def first_kernel(all_layers, total, count, where, order, tiles, edge_one, edge_two, bundle,
                 bundle_edge, diag_own, forward, backward, *rest):
    chunks = [rest[count * k : count * (k + 1)] for k in range(3)]
    out, message, coef, diag, edge_tiles, arrived, values, packed, spec, inverse = rest[3 * count :]
    steps, rows, width = arrived.shape[1:]
    core, mine = where[0, 0], where[0, 3]
    local = steps // count
    for at, parts in ((1, chunks[0]), (2 - 2 * core, chunks[1]), (2 * core, chunks[2])):
        for k, part in enumerate(parts):
            arrived[at, pl.ds(lax.bitwise_xor(mine, k) * local, local)] = part[...]
    size = steps * GROUP * 4
    groups = rows // (GROUP * 4)
    for at in range(3):
        for group in range(0, groups, 2):
            both = [
                arrived[at, :, place * GROUP * 4 : (place + 1) * GROUP * 4].reshape(size, width)
                for place in range(group, min(group + 2, groups))
            ]
            moved = jnp.dot(
                order[...], jnp.concatenate(both, axis=1), preferred_element_type=jnp.float32
            ).astype(jnp.bfloat16)
            for k in range(len(both)):
                values[4 * at : 4 * at + 4, (group + k) * GROUP : (group + k + 1) * GROUP] = moved[
                    :, k * width : (k + 1) * width
                ].reshape(4, GROUP, steps, width)

    window = bundle.shape[0] // 3
    sublane = lax.broadcasted_iota(jnp.int32, (8, width), 0)

    def widened(row, pair):
        turned = jnp.where(core == 0, pltpu.roll(row, 2, 0), pltpu.roll(row, 6, 0))
        for k in range(2):
            turned = jnp.where(
                sublane == 6 * core + k, jnp.broadcast_to(pair[k : k + 1], (8, width)), turned
            )
        return turned

    for at in range(3):
        for place in range(window):
            coef[at, place] = widened(bundle[at * window + place], bundle_edge[at * window + place])
    diag[...] = widened(diag_own[...], bundle_edge[3 * window])
    edge_tiles[where[0, 4]] = edge_one[...]
    edge_tiles[1 - where[0, 4]] = edge_two[...]

    def write(element, state):
        out[element] = state

    weights_of = chooser(where, tiles, edge_tiles, total)
    newton(values, weights_of, coef, diag, forward, backward, packed, spec, inverse,
           where[0, 1], 0, all_layers, write)
    layers = out.shape[1]
    for at in range(2):
        message[at * (layers - 2) : (at + 1) * (layers - 2)] = out[2 * core + at, 1 : layers - 1]
        begin = 2 * (layers - 2) + at * (layers - 4)
        message[begin : begin + layers - 4] = out[2 - 2 * core + at, 2 : layers - 2]


def second_kernel(all_layers, total, count, where, order, tiles,
                  edge_tiles, coef, diag, forward, backward, own, beside, across, out,
                  values, packed, spec, inverse, solved):
    core, mine = where[0, 0], where[0, 3]
    layers, steps, width = own.shape[1:]
    values[4:8] = own[...]
    values[pl.ds(8 - 8 * core, 4)] = beside[...]
    for at in range(2):
        values[2 + 6 * core + at, 1 : layers - 1] = across[
            at * (layers - 2) : (at + 1) * (layers - 2)
        ]
        begin = 2 * (layers - 2) + at * (layers - 4)
        values[10 * core + at, 2 : layers - 2] = across[begin : begin + layers - 4]

    def write(element, state):
        solved[element] = state

    weights_of = chooser(where, tiles, edge_tiles, total)
    newton(values, weights_of, coef, diag, forward, backward, packed, spec, inverse,
           where[0, 1], 2, all_layers, write)
    size = steps * GROUP * 4
    local = steps // count
    half = count // 2
    for group in range(solved.shape[1] // GROUP):
        part = solved[:, group * GROUP : (group + 1) * GROUP].reshape(size, width)
        moved = jnp.dot(order[...], part, preferred_element_type=jnp.float32)
        moved = moved.astype(jnp.bfloat16).reshape(steps, GROUP * 4, width)
        cut = pl.ds(group * GROUP * 4, GROUP * 4)
        for goal in range(count):
            side = lax.bitwise_xor(goal // half, core)
            place = lax.bitwise_xor(goal % half, lax.rem(mine, half))
            out[side, pl.ds(place * local, local), cut] = moved[goal * local : (goal + 1) * local]


def last_kernel(count, where, order, *rest):
    parts, out = rest[:-1], rest[-1]
    steps, layers, elems, width = out.shape
    half = count // 2
    layers //= half
    mine = where[3]
    upper, lower = mine // half, lax.rem(mine, half)
    for k, part in enumerate(parts):
        both = [part[lax.bitwise_xor(upper, side)].reshape(-1, width) for side in range(2)]
        moved = jnp.dot(
            order[...], jnp.concatenate(both, axis=0), preferred_element_type=jnp.float32
        )
        place = lax.bitwise_xor(lower, k)
        out[:, pl.ds(place * layers, layers)] = moved.reshape(steps, layers, elems, width)


def call(kernel, out_shape, scratch, scalars, arrays, later_than=()):
    vmem = pl.BlockSpec(memory_space=pltpu.VMEM)
    return pl.pallas_call(
        kernel,
        out_shape=out_shape,
        in_specs=[pl.BlockSpec(memory_space=pltpu.SMEM)] * len(scalars)
        + [vmem] * len(arrays)
        + [pl.BlockSpec(memory_space=pl.ANY)] * len(later_than),
        out_specs=jax.tree.map(lambda _: vmem, out_shape),
        scratch_shapes=scratch,
        compiler_params=pltpu.CompilerParams(vmem_limit_bytes=32 * 1024 * 1024),
    )(*scalars, *arrays, *later_than)


def shards(state_guess, start_state, reaction, source, self_diag, tiles, neighbors):
    local_steps, local_layers, local_elems, width = state_guess.shape
    count = lax.axis_size("tm")
    sections = lax.axis_size("space")
    mine, core = lax.axis_index("tm"), lax.axis_index("layer")
    steps = local_steps * count
    all_layers = local_layers * 2
    chip_layers = all_layers // count
    window = -(-(chip_layers + 2 * APPLICATIONS) // GROUP) * GROUP
    half = local_elems // 2
    swap = [(0, 1), (1, 0)]
    circle = []
    for section in range(sections):
        one, other = 2 * section + 1, 2 * ((section + 1) % sections)
        circle += [(one, other), (other, one)]

    def over_core(array):
        return lax.ppermute(array, "layer", swap)

    def over_circle(array):
        return lax.ppermute(array, ("space", "layer"), circle)

    def exchanged(parts):
        return [parts[0]] + [
            lax.ppermute(parts[k], "tm", [(i, i ^ k) for i in range(count)])
            for k in range(1, count)
        ]

    def held(shape, dtype=jnp.bfloat16):
        return jax.ShapeDtypeStruct(shape, dtype)

    pair = state_guess.astype(jnp.bfloat16).reshape(local_steps, local_layers, 2, half, width)
    flat = (local_steps, local_layers * half, width)
    keep = lax.dynamic_index_in_dim(pair, core, 2, keepdims=False).reshape(flat)
    give = lax.dynamic_index_in_dim(pair, 1 - core, 2, keepdims=False).reshape(flat)
    got = over_core(give)
    below = jnp.zeros((local_steps, APPLICATIONS * half, width), jnp.bfloat16)
    above = jnp.zeros(
        (local_steps, (window - chip_layers - APPLICATIONS) * half, width), jnp.bfloat16
    )
    whole = jnp.concatenate(
        [below, jnp.where(core == 0, keep, got), jnp.where(core == 0, got, keep), above], 1
    )
    pieces = [
        lax.dynamic_slice_in_dim(
            whole, lax.bitwise_xor(mine, k) * (chip_layers * half), window * half, 1
        )
        for k in range(count)
    ]
    chunks = exchanged(pieces)
    across = [over_circle(chunk) for chunk in chunks]
    beside = [over_core(chunk) for chunk in chunks]

    section = lax.axis_index("space") * local_elems
    place = jnp.stack(
        [core, mine * chip_layers - APPLICATIONS, section, mine, lax.axis_index("group")]
    ).astype(jnp.int32)
    edge_one = over_circle(
        lax.dynamic_index_in_dim(tiles, 6 * core + lax.axis_index("group"), 0, keepdims=False)
    )
    edge_two = lax.ppermute(edge_one, "group", swap)
    fields = (start_state, reaction, source)
    others = [over_core(field) for field in fields]
    ids = neighbors.T
    bundle, bundle_edge = call(
        fields_kernel,
        (
            held((3 * window, local_elems, width), jnp.float32),
            held((3 * window + 3, 2, width), jnp.float32),
        ),
        [],
        [place],
        [*fields, *others, self_diag, ids],
        [chunks[1]],
    )
    bundle_edge = over_circle(bundle_edge)
    edge_ids = bundle_edge[3 * window + 1 :, :, :local_elems].reshape(4, local_elems)
    where = jnp.concatenate(
        [jnp.pad(place[None], ((0, 0), (0, local_elems - 5))), ids, edge_ids.astype(jnp.int32)], 0
    )

    forward, backward, _ = transform_tables(steps)
    order = np.zeros((4, GROUP, steps, steps, GROUP, 4), np.float32)
    for element in range(4):
        for layer in range(GROUP):
            order[element, layer, :, :, layer, element] = np.eye(steps)
    order = order.reshape(4 * GROUP * steps, steps * GROUP * 4)
    last = window - 8
    order_last = np.zeros(
        (local_steps, chip_layers, 2, half, 2, local_steps, last, half), np.float32
    )
    for step in range(local_steps):
        for layer in range(chip_layers):
            for side in range(2):
                order_last[step, layer, side, :, side, step, layer, :] = np.eye(half)
    order_last = order_last.reshape(local_steps * chip_layers * 2 * half, -1)

    def constant(matrix):
        return jnp.asarray(matrix.astype(jnp.bfloat16))

    def table(matrix, layers):
        return constant(np.kron(np.eye(layers), matrix))

    def scratch(layers):
        return [
            pltpu.VMEM((12, layers, steps, width), jnp.bfloat16),
            pltpu.VMEM((8, layers - 2, steps, width), jnp.bfloat16),
            pltpu.VMEM((4, layers - 2, steps, width), jnp.float32),
            pltpu.VMEM((4, 3, layers - 2, steps // 2, width), jnp.float32),
        ]

    total = local_elems * sections
    state, edge, coef, diag, edge_tiles = call(
        lambda *refs: first_kernel(all_layers, total, count, *refs),
        (
            held((4, window - 4, steps, width)),
            held((2 * (window - 6) + 2 * (window - 8), steps, width)),
            held((3, window, 8, width), jnp.float32),
            held((8, width), jnp.float32),
            held((2,) + tiles.shape[1:]),
        ),
        [pltpu.VMEM((3, steps, window * half, width), jnp.bfloat16)] + scratch(window),
        [where],
        [constant(order), tiles, edge_one, edge_two, bundle, bundle_edge, self_diag,
         table(forward, window - 2), table(backward, window - 4), *chunks, *beside, *across],
    )
    solved = call(
        lambda *refs: second_kernel(all_layers, total, count, *refs),
        held((2, steps // 2, last * half, width)),
        scratch(window - 4) + [pltpu.VMEM((4, last, steps, width), jnp.bfloat16)],
        [where],
        [constant(order.T), tiles, edge_tiles, coef, diag,
         table(forward, window - 6), table(backward, last),
         state, over_core(state), over_circle(edge)],
    )

    keep, got = solved[0], over_core(solved[1])
    parts = []
    for k in range(count // 2):
        cut = slice(k * local_steps, (k + 1) * local_steps)
        pairs = []
        for device in range(count):
            high, low = device // (count // 2), device % (count // 2)
            for side in range(2):
                goal = side * (count // 2) + (low ^ k)
                pairs.append((2 * device + side, 2 * goal + high))
        parts.append(lax.ppermute(jnp.stack([keep[cut], got[cut]]), ("tm", "layer"), pairs))
    return call(
        lambda *refs: last_kernel(count, *refs),
        held(state_guess.shape, jnp.float32),
        [],
        [place],
        [constant(order_last), *parts],
    )


def solution(mesh):
    in_specs = (
        P("tm", ("group", "layer"), "space", None),
        P(("group", "layer"), "space", None),
        P(("group", "layer"), "space", None),
        P(("group", "layer"), "space", None),
        P("space", None),
        P("space", None, None, None),
        P("space", None),
    )
    out_specs = P("tm", ("group", "layer"), "space", None)
    return jax.shard_map(shards, mesh=mesh, in_specs=in_specs, out_specs=out_specs, check_vma=False)
```

```python
import math

import jax
import jax.numpy as jnp
import numpy as np
from jax import lax
from jax.experimental import pallas as pl
from jax.experimental.pallas import tpu as pltpu
from jax.sharding import PartitionSpec as P

NEWTON = 2
APPLICATIONS = 2 * NEWTON
OFFSETS = (-2, -1, 1, 2)
GROUP = 4

corner_weight = 0.25


def transform_tables(steps):
    beta = corner_weight ** (1.0 / steps)
    half = steps // 2
    counter = np.arange(steps)
    angle = ((counter[:, None] * counter[None, :]) % steps) * (2.0 * math.pi / steps)
    rising = np.power(beta, counter)
    falling = np.power(beta, -counter.astype(np.float64)) / steps
    fwd_re = np.cos(angle) * rising[None, :]
    fwd_im = -np.sin(angle) * rising[None, :]
    back_re = np.cos(angle) * falling[:, None]
    back_im = -np.sin(angle) * falling[:, None]
    forward = np.concatenate([fwd_re[:half], fwd_re[half : half + 1], fwd_im[1:half]], 0)
    twice = np.where(np.arange(half) == 0, 1.0, 2.0)
    backward = np.concatenate(
        [
            back_re[:, :half] * twice,
            back_re[:, half : half + 1],
            back_im[:, 1:half] * 2.0,
        ],
        1,
    )
    phase = counter * (2.0 * math.pi / steps)
    eigen_re = 1.0 - beta * np.cos(phase)
    eigen_im = beta * np.sin(phase)
    low_re = eigen_re[:half]
    low_im = np.where(np.arange(half) == 0, 0.0, eigen_im[:half])
    high_re = np.concatenate([eigen_re[half : half + 1], eigen_re[1:half]])
    eigen = np.stack([low_re, low_im, high_re]).astype(np.float32)
    return forward, backward, eigen


def applied(array, at, low, count, across, along):
    steps, width = array.shape[2:]

    def rows(element, first):
        return array[element, first : first + count].reshape(count * steps, width)

    parts = [rows(at + offset, low) for offset in range(-2, 4)]
    level = jnp.dot(
        jnp.concatenate(parts, axis=1), across[...], preferred_element_type=jnp.float32
    )
    outs = []
    for k in range(2):
        both = jnp.concatenate([rows(at + k, low - 1), rows(at + k, low + 1)], axis=1)
        out = jnp.dot(both, along[k][...], preferred_element_type=jnp.float32)
        out = out + level[:, k * width : (k + 1) * width]
        outs.append(out.reshape(count, steps, width))
    return outs


def halves(inverse, element, rows, array):
    first, cross, last = (inverse[element, k, rows] for k in range(3))
    half = array.shape[1] // 2
    part_a, part_b = array[:, :half], array[:, half:]
    return jnp.concatenate(
        [first * part_a - cross * part_b, cross * part_a + last * part_b], axis=1
    )


def newton(values, across, along, coef, diag, inverse, forward, backward, packed, spec, window_at,
           write):
    layers, steps, width = values.shape[1:]
    wide, inner = layers - 2, layers - 4
    for pair in range(4):
        mid = pair in (1, 2)
        low, count = (1, wide) if mid else (2, inner)
        rows = slice(window_at + low, window_at + low + count)
        images = applied(
            values, 2 * pair + 2, low, count, across[pair], (along[2 * pair], along[2 * pair + 1])
        )
        rhs = []
        for k, image in enumerate(images):
            element = 2 * pair + k
            state = values[element + 2, low : low + count].astype(jnp.float32)
            start = coef[0, rows, element : element + 1, :]
            reaction = coef[1, rows, element : element + 1, :]
            source = coef[2, rows, element : element + 1, :]
            own = diag[element : element + 1, :][None]
            time = lax.broadcasted_iota(jnp.int32, (count, steps, width), 1)
            previous = jnp.where(time == 0, start, pltpu.roll(state, 1, 1))
            residual = (
                state - previous + own * state + image + reaction * state * state * state - source
            )
            rhs.append((-residual).astype(jnp.bfloat16).reshape(count * steps, width))
        cut = count * steps
        out = jnp.dot(
            forward[:cut, :cut], jnp.concatenate(rhs, axis=1), preferred_element_type=jnp.float32
        )
        out = out.astype(jnp.bfloat16).astype(jnp.float32)
        rows = slice(window_at + low - 1, window_at + low - 1 + count)
        for k in range(2):
            element = 2 * pair + k
            part = out[:, k * width : (k + 1) * width].reshape(count, steps, width)
            sol = halves(inverse, element, rows, part)
            packed[element, low - 1 : low - 1 + count] = sol.astype(jnp.bfloat16)
            if mid:
                spec[element - 2] = part
    rows = slice(window_at + 1, window_at + 1 + inner)
    for pair in (1, 2):
        images = applied(
            packed, 2 * pair, 1, inner, across[pair], (along[2 * pair], along[2 * pair + 1])
        )
        finals = []
        for k, image in enumerate(images):
            element = 2 * pair + k
            final = halves(inverse, element, rows, spec[element - 2, 1 : 1 + inner] - image)
            finals.append(final.astype(jnp.bfloat16).reshape(inner * steps, width))
        delta = jnp.dot(
            backward[...], jnp.concatenate(finals, axis=1), preferred_element_type=jnp.float32
        )
        delta = delta.astype(jnp.bfloat16).astype(jnp.float32)
        for k in range(2):
            element = 2 * pair + k
            part = delta[:, k * width : (k + 1) * width].reshape(inner, steps, width)
            state = values[element + 2, 2 : 2 + inner].astype(jnp.float32) + part
            write(element - 2, state.astype(jnp.bfloat16))


def chooser(where, tiles, edge_tiles, total):
    core, first = where[0, 0], where[0, 2]

    def blocks(table, ids, at, element, row):
        places = [0]
        for offset in OFFSETS:
            wanted = lax.rem(element + (offset + total), total)
            slot = jnp.int32(1)
            for column in range(1, 4):
                slot = jnp.where(where[ids + column, at] == wanted, column + 1, slot)
            places.append(slot)
        return [table[row, place] for place in places + [5, 6]]

    def weights_of(element):
        local = element - 2 + 4 * core
        number = first + local + total
        if 2 <= element < 6:
            return blocks(tiles, 1, local, number, local)
        outer = element if element < 2 else element - 6
        inside = element + 2 if element < 2 else element - 2
        here = blocks(tiles, 1, inside, number, inside)
        there = blocks(edge_tiles, 5, 6 - 6 * core + outer, number, outer)
        away = core == (0 if element < 2 else 1)
        return [jnp.where(away, two, one) for one, two in zip(here, there)]

    return weights_of


def lay_tiles(weights_of, pair, across, along, to_across, to_along):
    width = along.shape[-1]
    for k in range(2):
        own, two_before, before, behind, two_behind, below, above = weights_of(2 * pair + k)
        lanes = slice(k * width, (k + 1) * width)
        for at, block in enumerate((two_before, before, own, behind, two_behind)):
            across[to_across, (at + k) * width : (at + k + 1) * width, lanes] = block
        empty = 5 - 5 * k
        across[to_across, empty * width : (empty + 1) * width, lanes] = jnp.zeros_like(own)
        along[to_along + k, :width] = below
        along[to_along + k, width:] = above


def pack_kernel(start, reaction, source, _, fields):
    for at, field in enumerate((start, reaction, source)):
        fields[at] = field[...]


def fields_kernel(where, fields, others, diag, ids, _, bundle, edge):
    layers = fields.shape[1]
    core, base = where[0], where[1]
    window = bundle.shape[0] // 3
    for at in range(3):
        for place in range(window):
            layer = jnp.clip(base + place, 0, 2 * layers - 1)
            own = layer // layers == core
            layer = lax.rem(layer, layers)
            row = jnp.where(own, fields[at, layer], others[at, layer])
            bundle[at * window + place] = row
            edge[at * window + place] = jnp.where(core == 0, row[0:2], row[6:8])
    edge[3 * window] = jnp.where(core == 0, diag[0:2], diag[6:8])
    for at in range(2):
        edge[3 * window + 1 + at, :, 0:8] = ids[2 * at : 2 * at + 2].astype(jnp.float32)


def arrive(where, count, chunks, order, arrived, values, at_elements):
    core, mine = where[0, 0], where[0, 3]
    steps, rows, width = arrived.shape
    local = steps // count
    for k, part in enumerate(chunks):
        arrived[pl.ds(lax.bitwise_xor(mine, k) * local, local)] = part[...]
    size = steps * GROUP * 4
    groups = rows // (GROUP * 4)
    for group in range(0, groups, 2):
        both = [
            arrived[:, place * GROUP * 4 : (place + 1) * GROUP * 4].reshape(size, width)
            for place in range(group, min(group + 2, groups))
        ]
        moved = jnp.dot(
            order[...], jnp.concatenate(both, axis=1), preferred_element_type=jnp.float32
        ).astype(jnp.bfloat16)
        for k in range(len(both)):
            values[pl.ds(at_elements, 4), (group + k) * GROUP : (group + k + 1) * GROUP] = moved[
                :, k * width : (k + 1) * width
            ].reshape(4, GROUP, steps, width)


def ready_kernel(all_layers, total, count, where, order, tiles, bundle, bundle_edge, diag_own,
                 *rest):
    own, beside = rest[:count], rest[count : 2 * count]
    coef, diag, inverse, values, across, along, arrived = rest[2 * count :]
    core, base = where[0, 0], where[0, 1]
    arrive(where, count, own, order, arrived, values, 4)
    arrive(where, count, beside, order, arrived, values, 8 - 8 * core)
    window = bundle.shape[0] // 3
    width = bundle.shape[2]
    sublane = lax.broadcasted_iota(jnp.int32, (8, width), 0)

    def widened(row, pair):
        turned = jnp.where(core == 0, pltpu.roll(row, 2, 0), pltpu.roll(row, 6, 0))
        for k in range(2):
            turned = jnp.where(
                sublane == 6 * core + k, jnp.broadcast_to(pair[k : k + 1], (8, width)), turned
            )
        return turned

    for at in range(3):
        for place in range(window):
            coef[at, place] = widened(bundle[at * window + place], bundle_edge[at * window + place])
    diag[...] = widened(diag_own[...], bundle_edge[3 * window])
    wide, half = inverse.shape[2:4]
    row = lax.broadcasted_iota(jnp.int32, (half, width), 0)
    eigen = []
    for numbers in transform_tables(2 * half)[2]:
        column = jnp.full((half, width), float(numbers[0]), jnp.float32)
        for at in range(1, half):
            column = jnp.where(row == at, float(numbers[at]), column)
        eigen.append(column)
    layer = lax.broadcasted_iota(jnp.int32, (wide, 1, width), 0) + (base + 1)
    inside = jnp.where((layer >= 0) & (layer < all_layers), 1.0, 0.0).astype(jnp.float32)
    for element in range(8):
        start = coef[0, 1 : 1 + wide, element : element + 1, :]
        reaction = coef[1, 1 : 1 + wide, element : element + 1, :]
        real = diag[element : element + 1, :][None] + 3.0 * reaction * start * start
        near = eigen[0][None] + real
        far = eigen[2][None] + real
        imag = eigen[1][None]
        near_over = inside / (near * near + imag * imag)
        inverse[element, 0] = near * near_over
        inverse[element, 1] = -imag * near_over
        inverse[element, 2] = far * (inside / (far * far + imag * imag))
    weights_of = chooser(where, tiles, None, total)
    for pair in (1, 2):
        lay_tiles(weights_of, pair, across, along, pair - 1, 2 * pair - 2)


class Joined:
    def __init__(self, outer, inner, each):
        self.outer, self.inner, self.each = outer, inner, each

    def __getitem__(self, at):
        if self.each <= at < 3 * self.each:
            return self.inner.at[at - self.each]
        return self.outer.at[at if at < self.each else at - 2 * self.each]


def first_kernel(total, count, where, order, tiles, edge_one, edge_two, coef, diag, inverse, ready,
                 inner_across, inner_along, forward, backward, *rest):
    chunks = rest[:count]
    out, message, across, along, edge_tiles, arrived, values, packed, spec = rest[count:]
    core, group = where[0, 0], where[0, 4]
    edge_tiles[group] = edge_one[...]
    edge_tiles[1 - group] = edge_two[...]
    weights_of = chooser(where, tiles, edge_tiles, total)
    lay_tiles(weights_of, 0, across, along, 0, 0)
    lay_tiles(weights_of, 3, across, along, 1, 2)
    values[4:8] = ready[4:8]
    values[pl.ds(8 - 8 * core, 4)] = ready[pl.ds(8 - 8 * core, 4)]
    arrive(where, count, chunks, order, arrived, values, 8 * core)

    def write(element, state):
        out[element] = state

    newton(values, Joined(across, inner_across, 1), Joined(along, inner_along, 2), coef, diag,
           inverse, forward, backward, packed, spec, 0, write)
    layers = out.shape[1]
    for at in range(2):
        message[at * (layers - 2) : (at + 1) * (layers - 2)] = out[2 * core + at, 1 : layers - 1]
        begin = 2 * (layers - 2) + at * (layers - 4)
        message[begin : begin + layers - 4] = out[2 - 2 * core + at, 2 : layers - 2]


def second_kernel(count, where, order, coef, diag, inverse, across, along, inner_across,
                  inner_along, forward, backward, own, beside, far, out, values, packed, spec,
                  solved):
    core, mine = where[0, 0], where[0, 3]
    layers, steps, width = own.shape[1:]
    values[4:8] = own[...]
    values[pl.ds(8 - 8 * core, 4)] = beside[...]
    for at in range(2):
        values[2 + 6 * core + at, 1 : layers - 1] = far[
            at * (layers - 2) : (at + 1) * (layers - 2)
        ]
        begin = 2 * (layers - 2) + at * (layers - 4)
        values[10 * core + at, 2 : layers - 2] = far[begin : begin + layers - 4]

    def write(element, state):
        solved[element] = state

    newton(values, Joined(across, inner_across, 1), Joined(along, inner_along, 2), coef, diag,
           inverse, forward, backward, packed, spec, 2, write)
    size = steps * GROUP * 4
    local = steps // count
    for group in range(solved.shape[1] // GROUP):
        part = solved[:, group * GROUP : (group + 1) * GROUP].reshape(size, width)
        moved = jnp.dot(order[...], part, preferred_element_type=jnp.float32)
        moved = moved.astype(jnp.bfloat16).reshape(steps, GROUP * 4, width)
        cut = pl.ds(group * GROUP * 4, GROUP * 4)
        for goal in range(count):
            side = lax.bitwise_xor(goal % 2, core)
            place = lax.bitwise_xor(goal // 2, mine // 2)
            out[side, pl.ds(place * local, local), cut] = moved[goal * local : (goal + 1) * local]


def last_kernel(count, where, order, *rest):
    parts, out = rest[:-1], rest[-1]
    steps, layers, elems, width = out.shape
    half = count // 2
    layers //= half
    mine = where[3]
    for k, part in enumerate(parts):
        both = [part[lax.bitwise_xor(lax.rem(mine, 2), side)].reshape(-1, width) for side in range(2)]
        moved = jnp.dot(
            order[...], jnp.concatenate(both, axis=0), preferred_element_type=jnp.float32
        )
        place = lax.bitwise_xor(mine // 2, k)
        out[:, pl.ds(place * layers, layers)] = moved.reshape(steps, layers, elems, width)


def call(kernel, out_shape, scratch, scalars, arrays, later_than=()):
    vmem = pl.BlockSpec(memory_space=pltpu.VMEM)
    return pl.pallas_call(
        kernel,
        out_shape=out_shape,
        in_specs=[pl.BlockSpec(memory_space=pltpu.SMEM)] * len(scalars)
        + [vmem] * len(arrays)
        + [pl.BlockSpec(memory_space=pl.ANY)] * len(later_than),
        out_specs=jax.tree.map(lambda _: vmem, out_shape),
        scratch_shapes=scratch,
        compiler_params=pltpu.CompilerParams(vmem_limit_bytes=32 * 1024 * 1024),
    )(*scalars, *arrays, *later_than)


def shards(state_guess, start_state, reaction, source, self_diag, tiles, neighbors):
    local_steps, local_layers, local_elems, width = state_guess.shape
    count = lax.axis_size("tm")
    sections = lax.axis_size("space")
    mine, core = lax.axis_index("tm"), lax.axis_index("layer")
    steps = local_steps * count
    all_layers = local_layers * 2
    chip_layers = all_layers // count

    def rank(device):
        return device % 2 * (count // 2) + device // 2

    window = -(-(chip_layers + 2 * APPLICATIONS) // GROUP) * GROUP
    half = local_elems // 2
    swap = [(0, 1), (1, 0)]
    circle = []
    for section in range(sections):
        one, other = 2 * section + 1, 2 * ((section + 1) % sections)
        circle += [(one, other), (other, one)]

    def over_core(array):
        return lax.ppermute(array, "layer", swap)

    def over_circle(array):
        return lax.ppermute(array, ("space", "layer"), circle)

    def exchanged(parts):
        return [parts[0]] + [
            lax.ppermute(parts[k], "tm", [(i, i ^ k) for i in range(count)])
            for k in range(1, count)
        ]

    def held(shape, dtype=jnp.bfloat16):
        return jax.ShapeDtypeStruct(shape, dtype)

    pair = state_guess.astype(jnp.bfloat16).reshape(local_steps, local_layers, 2, half, width)
    flat = (local_steps, local_layers * half, width)
    keep = lax.dynamic_index_in_dim(pair, core, 2, keepdims=False).reshape(flat)
    give = lax.dynamic_index_in_dim(pair, 1 - core, 2, keepdims=False).reshape(flat)
    got = over_core(give)
    below = jnp.zeros((local_steps, APPLICATIONS * half, width), jnp.bfloat16)
    above = jnp.zeros(
        (local_steps, (window - chip_layers - APPLICATIONS) * half, width), jnp.bfloat16
    )
    whole = jnp.concatenate(
        [below, jnp.where(core == 0, keep, got), jnp.where(core == 0, got, keep), above], 1
    )
    pieces = [
        lax.dynamic_slice_in_dim(
            whole, rank(lax.bitwise_xor(mine, k)) * (chip_layers * half), window * half, 1
        )
        for k in range(count)
    ]
    chunks = exchanged(pieces)
    across = [over_circle(chunk) for chunk in chunks]
    beside = [over_core(chunk) for chunk in chunks]

    section = lax.axis_index("space") * local_elems
    place = jnp.stack(
        [core, rank(mine) * chip_layers - APPLICATIONS, section, mine, lax.axis_index("group")]
    ).astype(jnp.int32)
    edge_one = over_circle(
        lax.dynamic_index_in_dim(tiles, 6 * core + lax.axis_index("group"), 0, keepdims=False)
    )
    edge_two = lax.ppermute(edge_one, "group", swap)
    fields = call(
        pack_kernel,
        held((3,) + start_state.shape, jnp.float32),
        [],
        [],
        [start_state, reaction, source],
        [pieces[1]],
    )
    ids = neighbors.T
    bundle, bundle_edge = call(
        fields_kernel,
        (
            held((3 * window, local_elems, width), jnp.float32),
            held((3 * window + 3, 2, width), jnp.float32),
        ),
        [],
        [place],
        [fields, over_core(fields), self_diag, ids],
        [chunks[1]],
    )
    bundle_edge = over_circle(bundle_edge)
    edge_ids = bundle_edge[3 * window + 1 :, :, :local_elems].reshape(4, local_elems)
    where = jnp.concatenate(
        [jnp.pad(place[None], ((0, 0), (0, local_elems - 5))), ids, edge_ids.astype(jnp.int32)], 0
    )

    forward, backward, _ = transform_tables(steps)
    order = np.zeros((4, GROUP, steps, steps, GROUP, 4), np.float32)
    for element in range(4):
        for layer in range(GROUP):
            order[element, layer, :, :, layer, element] = np.eye(steps)
    order = order.reshape(4 * GROUP * steps, steps * GROUP * 4)
    last = window - 8
    order_last = np.zeros(
        (local_steps, chip_layers, 2, half, 2, local_steps, last, half), np.float32
    )
    for step in range(local_steps):
        for layer in range(chip_layers):
            for side in range(2):
                order_last[step, layer, side, :, side, step, layer, :] = np.eye(half)
    order_last = order_last.reshape(local_steps * chip_layers * 2 * half, -1)

    def constant(matrix):
        return jnp.asarray(matrix.astype(jnp.bfloat16))

    def table(matrix, layers):
        return constant(np.kron(np.eye(layers), matrix))

    def scratch(layers):
        return [
            pltpu.VMEM((12, layers, steps, width), jnp.bfloat16),
            pltpu.VMEM((8, layers - 2, steps, width), jnp.bfloat16),
            pltpu.VMEM((4, layers - 2, steps, width), jnp.float32),
        ]

    total = local_elems * sections
    two_across, four_along = held((2, 6 * width, 2 * width)), held((4, 2 * width, width))
    arrived = pltpu.VMEM((steps, window * half, width), jnp.bfloat16)
    coef, diag, inverse, ready, inner_across, inner_along = call(
        lambda *refs: ready_kernel(all_layers, total, count, *refs),
        (
            held((3, window, 8, width), jnp.float32),
            held((8, width), jnp.float32),
            held((8, 3, window - 2, steps // 2, width), jnp.float32),
            held((12, window, steps, width)),
            two_across,
            four_along,
        ),
        [arrived],
        [where],
        [constant(order), tiles, bundle, bundle_edge, self_diag, *chunks, *beside],
    )
    state, edge, outer_across, outer_along = call(
        lambda *refs: first_kernel(total, count, *refs),
        (
            held((4, window - 4, steps, width)),
            held((2 * (window - 6) + 2 * (window - 8), steps, width)),
            two_across,
            four_along,
        ),
        [pltpu.VMEM((2,) + tiles.shape[1:], jnp.bfloat16), arrived] + scratch(window),
        [where],
        [constant(order), tiles, edge_one, edge_two, coef, diag, inverse, ready, inner_across,
         inner_along, table(forward, window - 2), table(backward, window - 4), *across],
    )
    solved = call(
        lambda *refs: second_kernel(count, *refs),
        held((2, steps // 2, last * half, width)),
        scratch(window - 4) + [pltpu.VMEM((4, last, steps, width), jnp.bfloat16)],
        [where],
        [constant(order.T), coef, diag, inverse, outer_across, outer_along, inner_across,
         inner_along, table(forward, window - 6), table(backward, last),
         state, over_core(state), over_circle(edge)],
    )

    keep, got = solved[0], over_core(solved[1])
    parts = []
    for k in range(count // 2):
        cut = slice(k * local_steps, (k + 1) * local_steps)
        pairs = []
        for device in range(count):
            for side in range(2):
                goal = 2 * (device // 2 ^ k) + side
                pairs.append((2 * device + side, 2 * goal + device % 2))
        parts.append(lax.ppermute(jnp.stack([keep[cut], got[cut]]), ("tm", "layer"), pairs))
    return call(
        lambda *refs: last_kernel(count, *refs),
        held(state_guess.shape, jnp.float32),
        [],
        [place],
        [constant(order_last), *parts],
    )


def solution(mesh):
    in_specs = (
        P("tm", ("group", "layer"), "space", None),
        P(("group", "layer"), "space", None),
        P(("group", "layer"), "space", None),
        P(("group", "layer"), "space", None),
        P("space", None),
        P("space", None, None, None),
        P("space", None),
    )
    out_specs = P("tm", ("group", "layer"), "space", None)
    return jax.shard_map(shards, mesh=mesh, in_specs=in_specs, out_specs=out_specs, check_vma=False)
```

```python
import math

import jax
import jax.numpy as jnp
import numpy as np
from jax import lax
from jax.experimental import pallas as pl
from jax.experimental.pallas import tpu as pltpu
from jax.sharding import PartitionSpec as P

NEWTON = 2
APPLICATIONS = 2 * NEWTON
OFFSETS = (-2, -1, 1, 2)
GROUP = 4
OVER_GROUP = 3

corner_weight = 0.25


def chip_rank(device, count):
    return device % 2 * (count // 2) + device // 2


def transform_tables(steps):
    beta = corner_weight ** (1.0 / steps)
    half = steps // 2
    counter = np.arange(steps)
    angle = ((counter[:, None] * counter[None, :]) % steps) * (2.0 * math.pi / steps)
    rising = np.power(beta, counter)
    falling = np.power(beta, -counter.astype(np.float64)) / steps
    fwd_re = np.cos(angle) * rising[None, :]
    fwd_im = -np.sin(angle) * rising[None, :]
    back_re = np.cos(angle) * falling[:, None]
    back_im = -np.sin(angle) * falling[:, None]
    forward = np.concatenate([fwd_re[:half], fwd_re[half : half + 1], fwd_im[1:half]], 0)
    twice = np.where(np.arange(half) == 0, 1.0, 2.0)
    backward = np.concatenate(
        [
            back_re[:, :half] * twice,
            back_re[:, half : half + 1],
            back_im[:, 1:half] * 2.0,
        ],
        1,
    )
    phase = counter * (2.0 * math.pi / steps)
    eigen_re = 1.0 - beta * np.cos(phase)
    eigen_im = beta * np.sin(phase)
    low_re = eigen_re[:half]
    low_im = np.where(np.arange(half) == 0, 0.0, eigen_im[:half])
    high_re = np.concatenate([eigen_re[half : half + 1], eigen_re[1:half]])
    eigen = np.stack([low_re, low_im, high_re]).astype(np.float32)
    return forward, backward, eigen


def applied(array, at, low, count, across, along):
    steps, width = array.shape[2:]

    def rows(element, first):
        return array[element, first : first + count].reshape(count * steps, width)

    parts = [rows(at + offset, low) for offset in range(-2, 4)]
    level = jnp.dot(
        jnp.concatenate(parts, axis=1), across[...], preferred_element_type=jnp.float32
    )
    outs = []
    for k in range(2):
        both = jnp.concatenate([rows(at + k, low - 1), rows(at + k, low + 1)], axis=1)
        out = jnp.dot(both, along[k][...], preferred_element_type=jnp.float32)
        out = out + level[:, k * width : (k + 1) * width]
        outs.append(out.reshape(count, steps, width))
    return outs


def halves(inverse, element, rows, array):
    first, cross, last = (inverse[element, k, rows] for k in range(3))
    half = array.shape[1] // 2
    part_a, part_b = array[:, :half], array[:, half:]
    return jnp.concatenate(
        [first * part_a - cross * part_b, cross * part_a + last * part_b], axis=1
    )


def newton(values, across, along, coef, diag, inverse, forward, backward, packed, spec, window_at,
           write):
    layers, steps, width = values.shape[1:]
    wide, inner = layers - 2, layers - 4
    for pair in range(4):
        mid = pair in (1, 2)
        low, count = (1, wide) if mid else (2, inner)
        rows = slice(window_at + low, window_at + low + count)
        images = applied(
            values, 2 * pair + 2, low, count, across[pair], (along[2 * pair], along[2 * pair + 1])
        )
        rhs = []
        for k, image in enumerate(images):
            element = 2 * pair + k
            state = values[element + 2, low : low + count].astype(jnp.float32)
            start = coef[0, rows, element : element + 1, :]
            reaction = coef[1, rows, element : element + 1, :]
            source = coef[2, rows, element : element + 1, :]
            own = diag[element : element + 1, :][None]
            time = lax.broadcasted_iota(jnp.int32, (count, steps, width), 1)
            previous = jnp.where(time == 0, start, pltpu.roll(state, 1, 1))
            residual = (
                state - previous + own * state + image + reaction * state * state * state - source
            )
            rhs.append((-residual).astype(jnp.bfloat16).reshape(count * steps, width))
        cut = count * steps
        out = jnp.dot(
            forward[:cut, :cut], jnp.concatenate(rhs, axis=1), preferred_element_type=jnp.float32
        )
        out = out.astype(jnp.bfloat16).astype(jnp.float32)
        rows = slice(window_at + low - 1, window_at + low - 1 + count)
        for k in range(2):
            element = 2 * pair + k
            part = out[:, k * width : (k + 1) * width].reshape(count, steps, width)
            sol = halves(inverse, element, rows, part)
            packed[element, low - 1 : low - 1 + count] = sol.astype(jnp.bfloat16)
            if mid:
                spec[element - 2] = part
    rows = slice(window_at + 1, window_at + 1 + inner)
    for pair in (1, 2):
        images = applied(
            packed, 2 * pair, 1, inner, across[pair], (along[2 * pair], along[2 * pair + 1])
        )
        finals = []
        for k, image in enumerate(images):
            element = 2 * pair + k
            final = halves(inverse, element, rows, spec[element - 2, 1 : 1 + inner] - image)
            finals.append(final.astype(jnp.bfloat16).reshape(inner * steps, width))
        delta = jnp.dot(
            backward[...], jnp.concatenate(finals, axis=1), preferred_element_type=jnp.float32
        )
        delta = delta.astype(jnp.bfloat16).astype(jnp.float32)
        for k in range(2):
            element = 2 * pair + k
            part = delta[:, k * width : (k + 1) * width].reshape(inner, steps, width)
            state = values[element + 2, 2 : 2 + inner].astype(jnp.float32) + part
            write(element - 2, state.astype(jnp.bfloat16))


def chooser(core, slots, tiles):
    def weights_of(element):
        row = element - 2 + 4 * core
        if element < 2:
            row = element + 2
        elif element > 5:
            row = element - 2
        places = [0] + [slots[at, row] for at in range(4)] + [5, 6]
        return [tiles[row, place] for place in places]

    return weights_of


def lay_tiles(weights_of, pair, across, along, to_across, to_along):
    width = along.shape[-1]
    for k in range(2):
        own, two_before, before, behind, two_behind, below, above = weights_of(2 * pair + k)
        lanes = slice(k * width, (k + 1) * width)
        for at, block in enumerate((two_before, before, own, behind, two_behind)):
            across[to_across, (at + k) * width : (at + k + 1) * width, lanes] = block
        empty = 5 - 5 * k
        across[to_across, empty * width : (empty + 1) * width, lanes] = jnp.zeros_like(own)
        along[to_along + k, :width] = below
        along[to_along + k, width:] = above


def trim_kernel(count, *rest):
    out = rest[-1]
    for k, piece in enumerate(rest[:count]):
        local, rows, _ = piece.shape
        out[k * local : (k + 1) * local] = piece[:, 4 : rows - 4]


def gather_kernel(*rest):
    parts, out = rest[:-1], rest[-1]
    local = parts[0].shape[0]
    mine = lax.axis_index("tm")
    for k, part in enumerate(parts):
        out[pl.ds(lax.bitwise_xor(mine, k) * local, local)] = part[...]


def pack_kernel(start, reaction, source, _, fields):
    for at, field in enumerate((start, reaction, source)):
        fields[at] = field[...]


def first_layer(count, all_layers):
    return chip_rank(lax.axis_index("tm"), count) * (all_layers // count) - APPLICATIONS


def fields_kernel(count, fields, others, diag, slots, _, bundle, edge):
    layers = fields.shape[1]
    core, base = lax.axis_index("layer"), first_layer(count, 2 * layers)
    window = bundle.shape[0] // 3
    for at in range(3):
        for place in range(window):
            layer = jnp.clip(base + place, 0, 2 * layers - 1)
            own = layer // layers == core
            layer = lax.rem(layer, layers)
            row = jnp.where(own, fields[at, layer], others[at, layer])
            bundle[at * window + place] = row
            edge[at * window + place] = jnp.where(core == 0, row[0:2], row[6:8])
    edge[3 * window] = jnp.where(core == 0, diag[0:2], diag[6:8])
    for at in range(2):
        edge[3 * window + 1 + at, :, 0:8] = slots[2 * at : 2 * at + 2].astype(jnp.float32)


def arrive(arrived, order, values, at_elements):
    steps, rows, width = arrived.shape
    size = steps * GROUP * 4
    groups = rows // (GROUP * 4)
    for group in range(0, groups, 2):
        both = [
            arrived[:, place * GROUP * 4 : (place + 1) * GROUP * 4].reshape(size, width)
            for place in range(group, min(group + 2, groups))
        ]
        moved = jnp.dot(
            order[...], jnp.concatenate(both, axis=1), preferred_element_type=jnp.float32
        ).astype(jnp.bfloat16)
        for k in range(len(both)):
            values[pl.ds(at_elements, 4), (group + k) * GROUP : (group + k + 1) * GROUP] = moved[
                :, k * width : (k + 1) * width
            ].reshape(4, GROUP, steps, width)


def edge_tiles_kernel(tiles, out):
    at, group = 6 * lax.axis_index("layer"), lax.axis_index("group")
    count = tiles.shape[1]
    out[:count] = tiles[at + group]
    out[count:] = tiles[at + 1 - group, : out.shape[0] - count]


def ready_kernel(all_layers, count, slots, order, tiles, bundle, bundle_edge, diag_own, own, beside,
                 coef, diag, inverse, values, across, along, picks):
    core, base = lax.axis_index("layer"), first_layer(count, all_layers)
    arrive(own, order, values, 4)
    arrive(beside, order, values, 8 - 8 * core)
    window = bundle.shape[0] // 3
    width = bundle.shape[2]
    sublane = lax.broadcasted_iota(jnp.int32, (8, width), 0)

    def widened(row, pair):
        turned = jnp.where(core == 0, pltpu.roll(row, 2, 0), pltpu.roll(row, 6, 0))
        for k in range(2):
            turned = jnp.where(
                sublane == 6 * core + k, jnp.broadcast_to(pair[k : k + 1], (8, width)), turned
            )
        return turned

    for at in range(3):
        for place in range(window):
            coef[at, place] = widened(bundle[at * window + place], bundle_edge[at * window + place])
    diag[...] = widened(diag_own[...], bundle_edge[3 * window])
    wide, half = inverse.shape[2:4]
    row = lax.broadcasted_iota(jnp.int32, (half, width), 0)
    eigen = []
    for numbers in transform_tables(2 * half)[2]:
        column = jnp.full((half, width), float(numbers[0]), jnp.float32)
        for at in range(1, half):
            column = jnp.where(row == at, float(numbers[at]), column)
        eigen.append(column)
    layer = lax.broadcasted_iota(jnp.int32, (wide, 1, width), 0) + (base + 1)
    inside = jnp.where((layer >= 0) & (layer < all_layers), 1.0, 0.0).astype(jnp.float32)
    for element in range(8):
        start = coef[0, 1 : 1 + wide, element : element + 1, :]
        reaction = coef[1, 1 : 1 + wide, element : element + 1, :]
        real = diag[element : element + 1, :][None] + 3.0 * reaction * start * start
        near = eigen[0][None] + real
        far = eigen[2][None] + real
        imag = eigen[1][None]
        near_over = inside / (near * near + imag * imag)
        inverse[element, 0] = near * near_over
        inverse[element, 1] = -imag * near_over
        inverse[element, 2] = far * (inside / (far * far + imag * imag))
    weights_of = chooser(core, slots, tiles)
    for pair in range(4):
        lay_tiles(weights_of, pair, across, along, pair, 2 * pair)
    for k in range(2):
        for at in range(4):
            for slot in range(4):
                hit = jnp.where(slots[4 + at, 6 - 6 * core + k] == slot + 1, 1.0, 0.0)
                picks[4 * (4 * k + at) + slot] = jnp.full((8, width), hit, jnp.float32)


def first_kernel(count, order, coef, diag, inverse, ready, near_across, near_along, picks, edge_one,
                 edge_two, forward, backward, first, others, out, message, across, along, edge_tiles,
                 arrived, values, packed, spec):
    core, mine, group = lax.axis_index("layer"), lax.axis_index("tm"), lax.axis_index("group")
    rest = 7 - edge_two.shape[0]
    edge_tiles[group] = edge_one[0:7]
    edge_tiles[1 - group, 0:rest] = edge_one[7 : 7 + rest]
    edge_tiles[1 - group, rest:7] = edge_two[...]
    across[...] = near_across[...]
    along[...] = near_along[...]

    def weights_of(element):
        blocks = [edge_tiles[element, 0]]
        for at in range(4):
            block = 0.0
            for slot in range(4):
                pick = picks[4 * (4 * element + at) + slot, 0:1].astype(jnp.bfloat16)
                block = block + edge_tiles[element, 1 + slot] * pick
            blocks.append(block)
        return blocks + [edge_tiles[element, 5], edge_tiles[element, 6]]

    lay_tiles(weights_of, 0, across, along, 3 * core, 6 * core)
    values[4:8] = ready[4:8]
    values[pl.ds(8 - 8 * core, 4)] = ready[pl.ds(8 - 8 * core, 4)]
    steps, rows, width = arrived.shape
    local = steps // count
    arrived[:, :4] = jnp.zeros((steps, 4, width), jnp.bfloat16)
    arrived[:, rows - 4 :] = jnp.zeros((steps, 4, width), jnp.bfloat16)
    for k in range(count):
        part = first[...] if k == 0 else others[(k - 1) * local : k * local]
        arrived[pl.ds(lax.bitwise_xor(mine, k) * local, local), 4 : rows - 4] = part
    arrive(arrived, order, values, 8 * core)

    def write(element, state):
        out[element] = state

    newton(values, [across.at[k] for k in range(4)], [along.at[k] for k in range(8)], coef, diag,
           inverse, forward, backward, packed, spec, 0, write)
    layers = out.shape[1]
    for at in range(2):
        message[at * (layers - 2) : (at + 1) * (layers - 2)] = out[2 * core + at, 1 : layers - 1]
        begin = 2 * (layers - 2) + at * (layers - 4)
        message[begin : begin + layers - 4] = out[2 - 2 * core + at, 2 : layers - 2]


def second_kernel(count, order, coef, diag, inverse, across, along, forward, backward, own, beside,
                  far, out, values, packed, spec, solved):
    core, mine = lax.axis_index("layer"), lax.axis_index("tm")
    layers, steps, width = own.shape[1:]
    values[4:8] = own[...]
    values[pl.ds(8 - 8 * core, 4)] = beside[...]
    for at in range(2):
        values[2 + 6 * core + at, 1 : layers - 1] = far[
            at * (layers - 2) : (at + 1) * (layers - 2)
        ]
        begin = 2 * (layers - 2) + at * (layers - 4)
        values[10 * core + at, 2 : layers - 2] = far[begin : begin + layers - 4]

    def write(element, state):
        solved[element] = state

    newton(values, [across.at[k] for k in range(4)], [along.at[k] for k in range(8)], coef, diag,
           inverse, forward, backward, packed, spec, 2, write)
    size = steps * GROUP * 4
    local = steps // count
    for group in range(solved.shape[1] // GROUP):
        part = solved[:, group * GROUP : (group + 1) * GROUP].reshape(size, width)
        moved = jnp.dot(order[...], part, preferred_element_type=jnp.float32)
        moved = moved.astype(jnp.bfloat16).reshape(steps, GROUP * 4, width)
        cut = pl.ds(group * GROUP * 4, GROUP * 4)
        for goal in range(count):
            side = lax.bitwise_xor(goal % 2, core)
            place = lax.bitwise_xor(goal // 2, mine // 2)
            out[side, pl.ds(place * local, local), cut] = moved[goal * local : (goal + 1) * local]


def last_kernel(count, order, *rest):
    parts, out = rest[:-1], rest[-1]
    steps, layers, elems, width = out.shape
    half = count // 2
    layers //= half
    mine = lax.axis_index("tm")
    for k, part in enumerate(parts):
        both = [part[lax.bitwise_xor(lax.rem(mine, 2), side)].reshape(-1, width) for side in range(2)]
        moved = jnp.dot(
            order[...], jnp.concatenate(both, axis=0), preferred_element_type=jnp.float32
        )
        place = lax.bitwise_xor(mine // 2, k)
        out[:, pl.ds(place * layers, layers)] = moved.reshape(steps, layers, elems, width)


def call(kernel, out_shape, scratch, scalars, arrays, later_than=()):
    vmem = pl.BlockSpec(memory_space=pltpu.VMEM)
    return pl.pallas_call(
        kernel,
        out_shape=out_shape,
        in_specs=[pl.BlockSpec(memory_space=pltpu.SMEM)] * len(scalars)
        + [vmem] * len(arrays)
        + [pl.BlockSpec(memory_space=pl.ANY)] * len(later_than),
        out_specs=jax.tree.map(lambda _: vmem, out_shape),
        scratch_shapes=scratch,
        compiler_params=pltpu.CompilerParams(vmem_limit_bytes=32 * 1024 * 1024),
    )(*scalars, *arrays, *later_than)


def shards(state_guess, start_state, reaction, source, self_diag, tiles, neighbors):
    local_steps, local_layers, local_elems, width = state_guess.shape
    count = lax.axis_size("tm")
    sections = lax.axis_size("space")
    mine, core = lax.axis_index("tm"), lax.axis_index("layer")
    steps = local_steps * count
    all_layers = local_layers * 2
    chip_layers = all_layers // count

    window = -(-(chip_layers + 2 * APPLICATIONS) // GROUP) * GROUP
    half = local_elems // 2
    swap = [(0, 1), (1, 0)]
    circle = []
    for section in range(sections):
        one, other = 2 * section + 1, 2 * ((section + 1) % sections)
        circle += [(one, other), (other, one)]

    def over_core(array):
        return lax.ppermute(array, "layer", swap)

    def over_circle(array):
        return lax.ppermute(array, ("space", "layer"), circle)

    def exchanged(parts):
        return [parts[0]] + [
            lax.ppermute(parts[k], "tm", [(i, i ^ k) for i in range(count)])
            for k in range(1, count)
        ]

    def held(shape, dtype=jnp.bfloat16):
        return jax.ShapeDtypeStruct(shape, dtype)

    pair = state_guess.astype(jnp.bfloat16).reshape(local_steps, local_layers, 2, half, width)
    flat = (local_steps, local_layers * half, width)
    keep = lax.dynamic_index_in_dim(pair, core, 2, keepdims=False).reshape(flat)
    give = lax.dynamic_index_in_dim(pair, 1 - core, 2, keepdims=False).reshape(flat)
    got = over_core(give)
    below = jnp.zeros((local_steps, APPLICATIONS * half, width), jnp.bfloat16)
    above = jnp.zeros(
        (local_steps, (window - chip_layers - APPLICATIONS) * half, width), jnp.bfloat16
    )
    whole = jnp.concatenate(
        [below, jnp.where(core == 0, keep, got), jnp.where(core == 0, got, keep), above], 1
    )
    pieces = [
        lax.dynamic_slice_in_dim(
            whole, chip_rank(lax.bitwise_xor(mine, k), count) * (chip_layers * half), window * half, 1
        )
        for k in range(count)
    ]
    chunks = exchanged(pieces)
    rest = tiles.shape[1] - OVER_GROUP
    edge_one = call(
        edge_tiles_kernel,
        held((tiles.shape[1] + rest,) + tiles.shape[2:]),
        [],
        [],
        [tiles],
    )
    edge_one = over_circle(edge_one)
    edge_two = lax.ppermute(edge_one[rest : tiles.shape[1]], "group", swap)
    def trimmed(parts, later_than):
        return call(
            lambda *refs: trim_kernel(len(parts), *refs),
            held((local_steps * len(parts), (window - 2) * half, width)),
            [],
            [],
            parts,
            later_than,
        )

    across = [over_circle(trimmed(chunks[:1], []))]
    across.append(over_circle(trimmed(chunks[1:], [across[0], edge_one])))

    own = call(
        gather_kernel, held((steps, window * half, width)), [], [], list(chunks)
    )

    fields = call(
        pack_kernel,
        held((3,) + start_state.shape, jnp.float32),
        [],
        [],
        [start_state, reaction, source],
        [pieces[1]],
    )
    total = local_elems * sections
    number = local_elems * lax.axis_index("space") + jnp.arange(local_elems, dtype=jnp.int32)
    wanted = (number[None] + jnp.array(OFFSETS, jnp.int32)[:, None] + total) % total
    ids = neighbors.T
    slots = 1 + sum(at * (ids[at : at + 1] == wanted).astype(jnp.int32) for at in range(1, 4))
    bundle, bundle_edge = call(
        lambda *refs: fields_kernel(count, *refs),
        (
            held((3 * window, local_elems, width), jnp.float32),
            held((3 * window + 3, 2, width), jnp.float32),
        ),
        [],
        [],
        [fields, over_core(fields), self_diag, slots],
        [chunks[1]],
    )
    bundle_edge = over_circle(bundle_edge)
    edge_slots = bundle_edge[3 * window + 1 :, :, :local_elems].reshape(4, local_elems)
    slots = jnp.concatenate([slots, edge_slots.astype(jnp.int32)], 0)

    forward, backward, _ = transform_tables(steps)
    order = np.zeros((4, GROUP, steps, steps, GROUP, 4), np.float32)
    for element in range(4):
        for layer in range(GROUP):
            order[element, layer, :, :, layer, element] = np.eye(steps)
    order = order.reshape(4 * GROUP * steps, steps * GROUP * 4)
    last = window - 8
    order_last = np.zeros(
        (local_steps, chip_layers, 2, half, 2, local_steps, last, half), np.float32
    )
    for step in range(local_steps):
        for layer in range(chip_layers):
            for side in range(2):
                order_last[step, layer, side, :, side, step, layer, :] = np.eye(half)
    order_last = order_last.reshape(local_steps * chip_layers * 2 * half, -1)

    def constant(matrix):
        return jnp.asarray(matrix.astype(jnp.bfloat16))

    def table(matrix, layers):
        return constant(np.kron(np.eye(layers), matrix))

    def scratch(layers):
        return [
            pltpu.VMEM((12, layers, steps, width), jnp.bfloat16),
            pltpu.VMEM((8, layers - 2, steps, width), jnp.bfloat16),
            pltpu.VMEM((4, layers - 2, steps, width), jnp.float32),
        ]

    total = local_elems * sections
    arrived = pltpu.VMEM((steps, window * half, width), jnp.bfloat16)
    laid = (held((4, 6 * width, 2 * width)), held((8, 2 * width, width)))
    coef, diag, inverse, ready, near_across, near_along, picks = call(
        lambda *refs: ready_kernel(all_layers, count, *refs),
        (
            held((3, window, 8, width), jnp.float32),
            held((8, width), jnp.float32),
            held((8, 3, window - 2, steps // 2, width), jnp.float32),
            held((12, window, steps, width)),
            *laid,
            held((32, 8, width), jnp.float32),
        ),
        [],
        [slots],
        [constant(order), tiles, bundle, bundle_edge, self_diag, own, over_core(own)],
    )
    state, edge, *laid = call(
        lambda *refs: first_kernel(count, *refs),
        (
            held((4, window - 4, steps, width)),
            held((2 * (window - 6) + 2 * (window - 8), steps, width)),
            *laid,
        ),
        [pltpu.VMEM((2,) + tiles.shape[1:], jnp.bfloat16), arrived] + scratch(window),
        [],
        [constant(order), coef, diag, inverse, ready, near_across, near_along, picks, edge_one,
         edge_two, table(forward, window - 2), table(backward, window - 4), *across],
    )
    solved = call(
        lambda *refs: second_kernel(count, *refs),
        held((2, steps // 2, last * half, width)),
        scratch(window - 4) + [pltpu.VMEM((4, last, steps, width), jnp.bfloat16)],
        [],
        [constant(order.T), coef, diag, inverse, *laid,
         table(forward, window - 6), table(backward, last),
         state, over_core(state), over_circle(edge)],
    )

    keep, got = solved[0], over_core(solved[1])
    parts = []
    for k in range(count // 2):
        cut = slice(k * local_steps, (k + 1) * local_steps)
        pairs = []
        for device in range(count):
            for side in range(2):
                goal = 2 * (device // 2 ^ k) + side
                pairs.append((2 * device + side, 2 * goal + device % 2))
        parts.append(lax.ppermute(jnp.stack([keep[cut], got[cut]]), ("tm", "layer"), pairs))
    return call(
        lambda *refs: last_kernel(count, *refs),
        held(state_guess.shape, jnp.float32),
        [],
        [],
        [constant(order_last), *parts],
    )


def solution(mesh):
    in_specs = (
        P("tm", ("group", "layer"), "space", None),
        P(("group", "layer"), "space", None),
        P(("group", "layer"), "space", None),
        P(("group", "layer"), "space", None),
        P("space", None),
        P("space", None, None, None),
        P("space", None),
    )
    out_specs = P("tm", ("group", "layer"), "space", None)
    return jax.shard_map(shards, mesh=mesh, in_specs=in_specs, out_specs=out_specs, check_vma=False)
```

```python
import math

import jax
import jax.numpy as jnp
import numpy as np
from jax import lax
from jax.experimental import pallas as pl
from jax.experimental.pallas import tpu as pltpu
from jax.sharding import PartitionSpec as P

NEWTON = 2
APPLICATIONS = 2 * NEWTON
OFFSETS = (-2, -1, 1, 2)
GROUP = 4
OVER_GROUP = 3

corner_weight = 0.25


def chip_rank(device, count):
    return device % 2 * (count // 2) + device // 2


def transform_tables(steps):
    beta = corner_weight ** (1.0 / steps)
    half = steps // 2
    counter = np.arange(steps)
    angle = ((counter[:, None] * counter[None, :]) % steps) * (2.0 * math.pi / steps)
    rising = np.power(beta, counter)
    falling = np.power(beta, -counter.astype(np.float64)) / steps
    fwd_re = np.cos(angle) * rising[None, :]
    fwd_im = -np.sin(angle) * rising[None, :]
    back_re = np.cos(angle) * falling[:, None]
    back_im = -np.sin(angle) * falling[:, None]
    forward = np.concatenate([fwd_re[:half], fwd_re[half : half + 1], fwd_im[1:half]], 0)
    twice = np.where(np.arange(half) == 0, 1.0, 2.0)
    backward = np.concatenate(
        [
            back_re[:, :half] * twice,
            back_re[:, half : half + 1],
            back_im[:, 1:half] * 2.0,
        ],
        1,
    )
    phase = counter * (2.0 * math.pi / steps)
    eigen_re = 1.0 - beta * np.cos(phase)
    eigen_im = beta * np.sin(phase)
    low_re = eigen_re[:half]
    low_im = np.where(np.arange(half) == 0, 0.0, eigen_im[:half])
    high_re = np.concatenate([eigen_re[half : half + 1], eigen_re[1:half]])
    eigen = np.stack([low_re, low_im, high_re]).astype(np.float32)
    return forward, backward, eigen


def applied(array, at, low, count, across, along):
    steps, width = array.shape[2:]

    def rows(element, first):
        return array[element, first : first + count].reshape(count * steps, width)

    parts = [rows(at + offset, low) for offset in range(-2, 4)]
    level = jnp.dot(
        jnp.concatenate(parts, axis=1), across[...], preferred_element_type=jnp.float32
    )
    outs = []
    for k in range(2):
        both = jnp.concatenate([rows(at + k, low - 1), rows(at + k, low + 1)], axis=1)
        out = jnp.dot(both, along[k][...], preferred_element_type=jnp.float32)
        out = out + level[:, k * width : (k + 1) * width]
        outs.append(out.reshape(count, steps, width))
    return outs


def halves(inverse, element, rows, array):
    first, cross, last = (inverse[element, k, rows] for k in range(3))
    half = array.shape[1] // 2
    part_a, part_b = array[:, :half], array[:, half:]
    return jnp.concatenate(
        [first * part_a - cross * part_b, cross * part_a + last * part_b], axis=1
    )


def newton(values, across, along, coef, diag, inverse, forward, backward, packed, spec, window_at,
           write):
    layers, steps, width = values.shape[1:]
    wide, inner = layers - 2, layers - 4
    for pair in range(4):
        mid = pair in (1, 2)
        low, count = (1, wide) if mid else (2, inner)
        rows = slice(window_at + low, window_at + low + count)
        images = applied(
            values, 2 * pair + 2, low, count, across[pair], (along[2 * pair], along[2 * pair + 1])
        )
        rhs = []
        for k, image in enumerate(images):
            element = 2 * pair + k
            state = values[element + 2, low : low + count].astype(jnp.float32)
            start = coef[0, rows, element : element + 1, :]
            reaction = coef[1, rows, element : element + 1, :]
            source = coef[2, rows, element : element + 1, :]
            own = diag[element : element + 1, :][None]
            time = lax.broadcasted_iota(jnp.int32, (count, steps, width), 1)
            previous = jnp.where(time == 0, start, pltpu.roll(state, 1, 1))
            residual = (
                state - previous + own * state + image + reaction * state * state * state - source
            )
            rhs.append((-residual).astype(jnp.bfloat16).reshape(count * steps, width))
        cut = count * steps
        out = jnp.dot(
            forward[:cut, :cut], jnp.concatenate(rhs, axis=1), preferred_element_type=jnp.float32
        )
        out = out.astype(jnp.bfloat16).astype(jnp.float32)
        rows = slice(window_at + low - 1, window_at + low - 1 + count)
        for k in range(2):
            element = 2 * pair + k
            part = out[:, k * width : (k + 1) * width].reshape(count, steps, width)
            sol = halves(inverse, element, rows, part)
            packed[element, low - 1 : low - 1 + count] = sol.astype(jnp.bfloat16)
            if mid:
                spec[element - 2] = part
    rows = slice(window_at + 1, window_at + 1 + inner)
    for pair in (1, 2):
        images = applied(
            packed, 2 * pair, 1, inner, across[pair], (along[2 * pair], along[2 * pair + 1])
        )
        finals = []
        for k, image in enumerate(images):
            element = 2 * pair + k
            final = halves(inverse, element, rows, spec[element - 2, 1 : 1 + inner] - image)
            finals.append(final.astype(jnp.bfloat16).reshape(inner * steps, width))
        delta = jnp.dot(
            backward[...], jnp.concatenate(finals, axis=1), preferred_element_type=jnp.float32
        )
        delta = delta.astype(jnp.bfloat16).astype(jnp.float32)
        for k in range(2):
            element = 2 * pair + k
            part = delta[:, k * width : (k + 1) * width].reshape(inner, steps, width)
            state = values[element + 2, 2 : 2 + inner].astype(jnp.float32) + part
            write(element - 2, state.astype(jnp.bfloat16))


def chooser(core, slots, tiles):
    def weights_of(element):
        row = element - 2 + 4 * core
        if element < 2:
            row = element + 2
        elif element > 5:
            row = element - 2
        places = [0] + [slots[at, row] for at in range(4)] + [5, 6]
        return [tiles[row, place] for place in places]

    return weights_of


def lay_tiles(weights_of, pair, across, along, to_across, to_along):
    width = along.shape[-1]
    for k in range(2):
        own, two_before, before, behind, two_behind, below, above = weights_of(2 * pair + k)
        lanes = slice(k * width, (k + 1) * width)
        for at, block in enumerate((two_before, before, own, behind, two_behind)):
            across[to_across, (at + k) * width : (at + k + 1) * width, lanes] = block
        empty = 5 - 5 * k
        across[to_across, empty * width : (empty + 1) * width, lanes] = jnp.zeros_like(own)
        along[to_along + k, :width] = below
        along[to_along + k, width:] = above


def trim_kernel(count, *rest):
    out = rest[-1]
    for k, piece in enumerate(rest[:count]):
        local, rows, _ = piece.shape
        out[k * local : (k + 1) * local] = piece[:, 4 : rows - 4]


def gather_kernel(*rest):
    parts, out = rest[:-1], rest[-1]
    local = parts[0].shape[0]
    mine = lax.axis_index("tm")
    for k, part in enumerate(parts):
        out[pl.ds(lax.bitwise_xor(mine, k) * local, local)] = part[...]


def pack_kernel(start, reaction, source, _, fields):
    for at, field in enumerate((start, reaction, source)):
        fields[at] = field[...]


def first_layer(count, all_layers):
    return chip_rank(lax.axis_index("tm"), count) * (all_layers // count) - APPLICATIONS


def fields_kernel(count, fields, others, diag, slots, _, bundle, edge):
    layers = fields.shape[1]
    core, base = lax.axis_index("layer"), first_layer(count, 2 * layers)
    window = bundle.shape[0] // 3
    for at in range(3):
        for place in range(window):
            layer = jnp.clip(base + place, 0, 2 * layers - 1)
            own = layer // layers == core
            layer = lax.rem(layer, layers)
            row = jnp.where(own, fields[at, layer], others[at, layer])
            bundle[at * window + place] = row
            edge[at * window + place] = jnp.where(core == 0, row[0:2], row[6:8])
    edge[3 * window] = jnp.where(core == 0, diag[0:2], diag[6:8])
    for at in range(2):
        edge[3 * window + 1 + at, :, 0:8] = slots[2 * at : 2 * at + 2].astype(jnp.float32)


def arrive(arrived, order, values, at_elements):
    steps, rows, width = arrived.shape
    size = steps * GROUP * 4
    groups = rows // (GROUP * 4)
    for group in range(0, groups, 2):
        both = [
            arrived[:, place * GROUP * 4 : (place + 1) * GROUP * 4].reshape(size, width)
            for place in range(group, min(group + 2, groups))
        ]
        moved = jnp.dot(
            order[...], jnp.concatenate(both, axis=1), preferred_element_type=jnp.float32
        ).astype(jnp.bfloat16)
        for k in range(len(both)):
            values[pl.ds(at_elements, 4), (group + k) * GROUP : (group + k + 1) * GROUP] = moved[
                :, k * width : (k + 1) * width
            ].reshape(4, GROUP, steps, width)


def edge_tiles_kernel(tiles, out):
    group = lax.axis_index("group")
    count = tiles.shape[1]
    out[:count] = tiles[group]
    out[count:] = tiles[1 - group, : out.shape[0] - count]


def ready_kernel(all_layers, count, slots, order, tiles, bundle, bundle_edge, diag_own, own, beside,
                 coef, diag, inverse, values, across, along, picks):
    core, base = lax.axis_index("layer"), first_layer(count, all_layers)
    arrive(own, order, values, 4)
    arrive(beside, order, values, 8 - 8 * core)
    window = bundle.shape[0] // 3
    width = bundle.shape[2]
    sublane = lax.broadcasted_iota(jnp.int32, (8, width), 0)

    def widened(row, pair):
        turned = jnp.where(core == 0, pltpu.roll(row, 2, 0), pltpu.roll(row, 6, 0))
        for k in range(2):
            turned = jnp.where(
                sublane == 6 * core + k, jnp.broadcast_to(pair[k : k + 1], (8, width)), turned
            )
        return turned

    for at in range(3):
        for place in range(window):
            coef[at, place] = widened(bundle[at * window + place], bundle_edge[at * window + place])
    diag[...] = widened(diag_own[...], bundle_edge[3 * window])
    wide, half = inverse.shape[2:4]
    row = lax.broadcasted_iota(jnp.int32, (half, width), 0)
    eigen = []
    for numbers in transform_tables(2 * half)[2]:
        column = jnp.full((half, width), float(numbers[0]), jnp.float32)
        for at in range(1, half):
            column = jnp.where(row == at, float(numbers[at]), column)
        eigen.append(column)
    layer = lax.broadcasted_iota(jnp.int32, (wide, 1, width), 0) + (base + 1)
    inside = jnp.where((layer >= 0) & (layer < all_layers), 1.0, 0.0).astype(jnp.float32)
    for element in range(8):
        start = coef[0, 1 : 1 + wide, element : element + 1, :]
        reaction = coef[1, 1 : 1 + wide, element : element + 1, :]
        real = diag[element : element + 1, :][None] + 3.0 * reaction * start * start
        near = eigen[0][None] + real
        far = eigen[2][None] + real
        imag = eigen[1][None]
        near_over = inside / (near * near + imag * imag)
        inverse[element, 0] = near * near_over
        inverse[element, 1] = -imag * near_over
        inverse[element, 2] = far * (inside / (far * far + imag * imag))
    weights_of = chooser(core, slots, tiles)
    for pair in range(4):
        lay_tiles(weights_of, pair, across, along, pair, 2 * pair)
    for k in range(2):
        for at in range(4):
            for slot in range(4):
                hit = jnp.where(slots[4 + at, 6 - 6 * core + k] == slot + 1, 1.0, 0.0)
                picks[4 * (4 * k + at) + slot] = jnp.full((8, width), hit, jnp.float32)


def joined(outer, every, each):
    inner = [every.at[k] for k in range(each, 3 * each)]
    outer = [outer.at[k] for k in range(2 * each)]
    return outer[:each] + inner + outer[each:]


def first_kernel(count, order, coef, diag, inverse, ready, near_across, near_along, picks, edge_one,
                 edge_two, forward, backward, first, others, out, message, across, along, edge_tiles,
                 arrived, values, packed, spec):
    core, mine, group = lax.axis_index("layer"), lax.axis_index("tm"), lax.axis_index("group")
    rest = 7 - edge_two.shape[0]
    edge_tiles[group] = edge_one[0:7]
    edge_tiles[1 - group, 0:rest] = edge_one[7 : 7 + rest]
    edge_tiles[1 - group, rest:7] = edge_two[...]
    across[1 - core] = near_across[3 - 3 * core]
    along[pl.ds(2 - 2 * core, 2)] = near_along[pl.ds(6 - 6 * core, 2)]

    def weights_of(element):
        blocks = [edge_tiles[element, 0]]
        for at in range(4):
            block = 0.0
            for slot in range(4):
                pick = picks[4 * (4 * element + at) + slot, 0:1].astype(jnp.bfloat16)
                block = block + edge_tiles[element, 1 + slot] * pick
            blocks.append(block)
        return blocks + [edge_tiles[element, 5], edge_tiles[element, 6]]

    lay_tiles(weights_of, 0, across, along, core, 2 * core)
    values[4:8] = ready[4:8]
    values[pl.ds(8 - 8 * core, 4)] = ready[pl.ds(8 - 8 * core, 4)]
    steps, rows, width = arrived.shape
    local = steps // count
    arrived[:, :4] = jnp.zeros((steps, 4, width), jnp.bfloat16)
    arrived[:, rows - 4 :] = jnp.zeros((steps, 4, width), jnp.bfloat16)
    for k in range(count):
        part = first[...] if k == 0 else others[(k - 1) * local : k * local]
        arrived[pl.ds(lax.bitwise_xor(mine, k) * local, local), 4 : rows - 4] = part
    arrive(arrived, order, values, 8 * core)

    def write(element, state):
        out[element] = state

    newton(values, joined(across, near_across, 1), joined(along, near_along, 2), coef, diag, inverse,
           forward, backward, packed, spec, 0, write)
    layers = out.shape[1]
    for at in range(2):
        message[at * (layers - 2) : (at + 1) * (layers - 2)] = out[2 * core + at, 1 : layers - 1]
        begin = 2 * (layers - 2) + at * (layers - 4)
        message[begin : begin + layers - 4] = out[2 - 2 * core + at, 2 : layers - 2]


def second_kernel(count, order, coef, diag, inverse, across, along, near_across, near_along,
                  forward, backward, own, beside, far, out, values, packed, spec, solved):
    core, mine = lax.axis_index("layer"), lax.axis_index("tm")
    layers, steps, width = own.shape[1:]
    values[4:8] = own[...]
    values[pl.ds(8 - 8 * core, 4)] = beside[...]
    for at in range(2):
        values[2 + 6 * core + at, 1 : layers - 1] = far[
            at * (layers - 2) : (at + 1) * (layers - 2)
        ]
        begin = 2 * (layers - 2) + at * (layers - 4)
        values[10 * core + at, 2 : layers - 2] = far[begin : begin + layers - 4]

    def write(element, state):
        solved[element] = state

    newton(values, joined(across, near_across, 1), joined(along, near_along, 2), coef, diag, inverse,
           forward, backward, packed, spec, 2, write)
    size = steps * GROUP * 4
    local = steps // count
    for group in range(solved.shape[1] // GROUP):
        part = solved[:, group * GROUP : (group + 1) * GROUP].reshape(size, width)
        moved = jnp.dot(order[...], part, preferred_element_type=jnp.float32)
        moved = moved.astype(jnp.bfloat16).reshape(steps, GROUP * 4, width)
        cut = pl.ds(group * GROUP * 4, GROUP * 4)
        for goal in range(count):
            side = lax.bitwise_xor(goal % 2, core)
            place = lax.bitwise_xor(goal // 2, mine // 2)
            out[side, pl.ds(place * local, local), cut] = moved[goal * local : (goal + 1) * local]


def last_kernel(count, order, *rest):
    parts, out = rest[:-1], rest[-1]
    steps, layers, elems, width = out.shape
    half = count // 2
    layers //= half
    mine = lax.axis_index("tm")
    for k, part in enumerate(parts):
        both = [part[lax.bitwise_xor(lax.rem(mine, 2), side)].reshape(-1, width) for side in range(2)]
        moved = jnp.dot(
            order[...], jnp.concatenate(both, axis=0), preferred_element_type=jnp.float32
        )
        place = lax.bitwise_xor(mine // 2, k)
        out[:, pl.ds(place * layers, layers)] = moved.reshape(steps, layers, elems, width)


def call(kernel, out_shape, scratch, scalars, arrays, later_than=()):
    vmem = pl.BlockSpec(memory_space=pltpu.VMEM)
    return pl.pallas_call(
        kernel,
        out_shape=out_shape,
        in_specs=[pl.BlockSpec(memory_space=pltpu.SMEM)] * len(scalars)
        + [vmem] * len(arrays)
        + [pl.BlockSpec(memory_space=pl.ANY)] * len(later_than),
        out_specs=jax.tree.map(lambda _: vmem, out_shape),
        scratch_shapes=scratch,
        compiler_params=pltpu.CompilerParams(vmem_limit_bytes=32 * 1024 * 1024),
    )(*scalars, *arrays, *later_than)


def shards(state_guess, start_state, reaction, source, self_diag, tiles, neighbors):
    local_steps, local_layers, local_elems, width = state_guess.shape
    count = lax.axis_size("tm")
    sections = lax.axis_size("space")
    mine, core = lax.axis_index("tm"), lax.axis_index("layer")
    steps = local_steps * count
    all_layers = local_layers * 2
    chip_layers = all_layers // count

    window = -(-(chip_layers + 2 * APPLICATIONS) // GROUP) * GROUP
    half = local_elems // 2
    swap = [(0, 1), (1, 0)]
    circle = []
    for section in range(sections):
        one, other = 2 * section + 1, 2 * ((section + 1) % sections)
        circle += [(one, other), (other, one)]

    def over_core(array):
        return lax.ppermute(array, "layer", swap)

    def over_circle(array):
        return lax.ppermute(array, ("space", "layer"), circle)

    def exchanged(parts):
        return [parts[0]] + [
            lax.ppermute(parts[k], "tm", [(i, i ^ k) for i in range(count)])
            for k in range(1, count)
        ]

    def held(shape, dtype=jnp.bfloat16):
        return jax.ShapeDtypeStruct(shape, dtype)

    pair = state_guess.astype(jnp.bfloat16).reshape(local_steps, local_layers, 2, half, width)
    flat = (local_steps, local_layers * half, width)
    keep = lax.dynamic_index_in_dim(pair, core, 2, keepdims=False).reshape(flat)
    give = lax.dynamic_index_in_dim(pair, 1 - core, 2, keepdims=False).reshape(flat)
    got = over_core(give)
    below = jnp.zeros((local_steps, APPLICATIONS * half, width), jnp.bfloat16)
    above = jnp.zeros(
        (local_steps, (window - chip_layers - APPLICATIONS) * half, width), jnp.bfloat16
    )
    whole = jnp.concatenate(
        [below, jnp.where(core == 0, keep, got), jnp.where(core == 0, got, keep), above], 1
    )
    pieces = [
        lax.dynamic_slice_in_dim(
            whole, chip_rank(lax.bitwise_xor(mine, k), count) * (chip_layers * half), window * half, 1
        )
        for k in range(count)
    ]
    chunks = exchanged(pieces)
    rest = tiles.shape[1] - OVER_GROUP
    edge_one = call(
        edge_tiles_kernel,
        held((tiles.shape[1] + rest,) + tiles.shape[2:]),
        [],
        [],
        [lax.dynamic_slice_in_dim(tiles, 6 * core, 2, 0)],
    )
    edge_one = over_circle(edge_one)
    edge_two = lax.ppermute(edge_one[rest : tiles.shape[1]], "group", swap)
    def trimmed(parts, later_than):
        return call(
            lambda *refs: trim_kernel(len(parts), *refs),
            held((local_steps * len(parts), (window - 2) * half, width)),
            [],
            [],
            parts,
            later_than,
        )

    across = [over_circle(trimmed(chunks[:1], []))]
    across.append(over_circle(trimmed(chunks[1:], [across[0], edge_one])))

    own = call(
        gather_kernel, held((steps, window * half, width)), [], [], list(chunks)
    )

    fields = call(
        pack_kernel,
        held((3,) + start_state.shape, jnp.float32),
        [],
        [],
        [start_state, reaction, source],
        [pieces[1]],
    )
    total = local_elems * sections
    number = local_elems * lax.axis_index("space") + jnp.arange(local_elems, dtype=jnp.int32)
    wanted = (number[None] + jnp.array(OFFSETS, jnp.int32)[:, None] + total) % total
    ids = neighbors.T
    slots = 1 + sum(at * (ids[at : at + 1] == wanted).astype(jnp.int32) for at in range(1, 4))
    bundle, bundle_edge = call(
        lambda *refs: fields_kernel(count, *refs),
        (
            held((3 * window, local_elems, width), jnp.float32),
            held((3 * window + 3, 2, width), jnp.float32),
        ),
        [],
        [],
        [fields, over_core(fields), self_diag, slots],
        [chunks[1]],
    )
    bundle_edge = over_circle(bundle_edge)
    edge_slots = bundle_edge[3 * window + 1 :, :, :local_elems].reshape(4, local_elems)
    slots = jnp.concatenate([slots, edge_slots.astype(jnp.int32)], 0)

    forward, backward, _ = transform_tables(steps)
    order = np.zeros((4, GROUP, steps, steps, GROUP, 4), np.float32)
    for element in range(4):
        for layer in range(GROUP):
            order[element, layer, :, :, layer, element] = np.eye(steps)
    order = order.reshape(4 * GROUP * steps, steps * GROUP * 4)
    last = window - 8
    order_last = np.zeros(
        (local_steps, chip_layers, 2, half, 2, local_steps, last, half), np.float32
    )
    for step in range(local_steps):
        for layer in range(chip_layers):
            for side in range(2):
                order_last[step, layer, side, :, side, step, layer, :] = np.eye(half)
    order_last = order_last.reshape(local_steps * chip_layers * 2 * half, -1)

    def constant(matrix):
        return jnp.asarray(matrix.astype(jnp.bfloat16))

    def table(matrix, layers):
        return constant(np.kron(np.eye(layers), matrix))

    def scratch(layers):
        return [
            pltpu.VMEM((12, layers, steps, width), jnp.bfloat16),
            pltpu.VMEM((8, layers - 2, steps, width), jnp.bfloat16),
            pltpu.VMEM((4, layers - 2, steps, width), jnp.float32),
        ]

    total = local_elems * sections
    arrived = pltpu.VMEM((steps, window * half, width), jnp.bfloat16)
    laid = (held((4, 6 * width, 2 * width)), held((8, 2 * width, width)))
    coef, diag, inverse, ready, near_across, near_along, picks = call(
        lambda *refs: ready_kernel(all_layers, count, *refs),
        (
            held((3, window, 8, width), jnp.float32),
            held((8, width), jnp.float32),
            held((8, 3, window - 2, steps // 2, width), jnp.float32),
            held((12, window, steps, width)),
            *laid,
            held((32, 8, width), jnp.float32),
        ),
        [],
        [slots],
        [constant(order), tiles, bundle, bundle_edge, self_diag, own, over_core(own)],
    )
    state, edge, *outer = call(
        lambda *refs: first_kernel(count, *refs),
        (
            held((4, window - 4, steps, width)),
            held((2 * (window - 6) + 2 * (window - 8), steps, width)),
            held((2, 6 * width, 2 * width)),
            held((4, 2 * width, width)),
        ),
        [pltpu.VMEM((2,) + tiles.shape[1:], jnp.bfloat16), arrived] + scratch(window),
        [],
        [constant(order), coef, diag, inverse, ready, near_across, near_along, picks, edge_one,
         edge_two, table(forward, window - 2), table(backward, window - 4), *across],
    )
    solved = call(
        lambda *refs: second_kernel(count, *refs),
        held((2, steps // 2, last * half, width)),
        scratch(window - 4) + [pltpu.VMEM((4, last, steps, width), jnp.bfloat16)],
        [],
        [constant(order.T), coef, diag, inverse, *outer, near_across, near_along,
         table(forward, window - 6), table(backward, last),
         state, over_core(state), over_circle(edge)],
    )

    keep, got = solved[0], over_core(solved[1])
    parts = []
    for k in range(count // 2):
        cut = slice(k * local_steps, (k + 1) * local_steps)
        pairs = []
        for device in range(count):
            for side in range(2):
                goal = 2 * (device // 2 ^ k) + side
                pairs.append((2 * device + side, 2 * goal + device % 2))
        parts.append(lax.ppermute(jnp.stack([keep[cut], got[cut]]), ("tm", "layer"), pairs))
    return call(
        lambda *refs: last_kernel(count, *refs),
        held(state_guess.shape, jnp.float32),
        [],
        [],
        [constant(order_last), *parts],
    )


def solution(mesh):
    in_specs = (
        P("tm", ("group", "layer"), "space", None),
        P(("group", "layer"), "space", None),
        P(("group", "layer"), "space", None),
        P(("group", "layer"), "space", None),
        P("space", None),
        P("space", None, None, None),
        P("space", None),
    )
    out_specs = P("tm", ("group", "layer"), "space", None)
    return jax.shard_map(shards, mesh=mesh, in_specs=in_specs, out_specs=out_specs, check_vma=False)
```

```python
import math

import jax
import jax.numpy as jnp
import numpy as np
from jax import lax
from jax.experimental import pallas as pl
from jax.experimental.pallas import tpu as pltpu
from jax.sharding import PartitionSpec as P

NEWTON = 2
APPLICATIONS = 2 * NEWTON
OFFSETS = (-2, -1, 1, 2)
GROUP = 4
OVER_GROUP = 3

corner_weight = 0.25


def chip_rank(device, count):
    return device % 2 * (count // 2) + device // 2


def transform_tables(steps):
    beta = corner_weight ** (1.0 / steps)
    half = steps // 2
    counter = np.arange(steps)
    angle = ((counter[:, None] * counter[None, :]) % steps) * (2.0 * math.pi / steps)
    rising = np.power(beta, counter)
    falling = np.power(beta, -counter.astype(np.float64)) / steps
    fwd_re = np.cos(angle) * rising[None, :]
    fwd_im = -np.sin(angle) * rising[None, :]
    back_re = np.cos(angle) * falling[:, None]
    back_im = -np.sin(angle) * falling[:, None]
    forward = np.concatenate([fwd_re[:half], fwd_re[half : half + 1], fwd_im[1:half]], 0)
    twice = np.where(np.arange(half) == 0, 1.0, 2.0)
    backward = np.concatenate(
        [
            back_re[:, :half] * twice,
            back_re[:, half : half + 1],
            back_im[:, 1:half] * 2.0,
        ],
        1,
    )
    phase = counter * (2.0 * math.pi / steps)
    eigen_re = 1.0 - beta * np.cos(phase)
    eigen_im = beta * np.sin(phase)
    low_re = eigen_re[:half]
    low_im = np.where(np.arange(half) == 0, 0.0, eigen_im[:half])
    high_re = np.concatenate([eigen_re[half : half + 1], eigen_re[1:half]])
    eigen = np.stack([low_re, low_im, high_re]).astype(np.float32)
    return forward, backward, eigen


def applied(array, at, low, count, across, along):
    steps, width = array.shape[2:]

    def rows(element, first):
        return array[element, first : first + count].reshape(count * steps, width)

    parts = [rows(at + offset, low) for offset in range(-2, 4)]
    level = jnp.dot(
        jnp.concatenate(parts, axis=1), across[...], preferred_element_type=jnp.float32
    )
    outs = []
    for k in range(2):
        both = jnp.concatenate([rows(at + k, low - 1), rows(at + k, low + 1)], axis=1)
        out = jnp.dot(both, along[k][...], preferred_element_type=jnp.float32)
        out = out + level[:, k * width : (k + 1) * width]
        outs.append(out.reshape(count, steps, width))
    return outs


def halves(inverse, element, rows, array):
    first, cross, last = (inverse[element, k, rows] for k in range(3))
    half = array.shape[1] // 2
    part_a, part_b = array[:, :half], array[:, half:]
    return jnp.concatenate(
        [first * part_a - cross * part_b, cross * part_a + last * part_b], axis=1
    )


def newton(values, across, along, coef, diag, inverse, forward, backward, packed, spec, window_at,
           write):
    layers, steps, width = values.shape[1:]
    wide, inner = layers - 2, layers - 4
    for pair in range(4):
        mid = pair in (1, 2)
        low, count = (1, wide) if mid else (2, inner)
        rows = slice(window_at + low, window_at + low + count)
        images = applied(
            values, 2 * pair + 2, low, count, across[pair], (along[2 * pair], along[2 * pair + 1])
        )
        rhs = []
        for k, image in enumerate(images):
            element = 2 * pair + k
            state = values[element + 2, low : low + count].astype(jnp.float32)
            start = coef[0, rows, element : element + 1, :]
            reaction = coef[1, rows, element : element + 1, :]
            source = coef[2, rows, element : element + 1, :]
            own = diag[element : element + 1, :][None]
            time = lax.broadcasted_iota(jnp.int32, (count, steps, width), 1)
            previous = jnp.where(time == 0, start, pltpu.roll(state, 1, 1))
            residual = (
                state - previous + own * state + image + reaction * state * state * state - source
            )
            rhs.append((-residual).astype(jnp.bfloat16).reshape(count * steps, width))
        cut = count * steps
        out = jnp.dot(
            forward[:cut, :cut], jnp.concatenate(rhs, axis=1), preferred_element_type=jnp.float32
        )
        out = out.astype(jnp.bfloat16).astype(jnp.float32)
        rows = slice(window_at + low - 1, window_at + low - 1 + count)
        for k in range(2):
            element = 2 * pair + k
            part = out[:, k * width : (k + 1) * width].reshape(count, steps, width)
            sol = halves(inverse, element, rows, part)
            packed[element, low - 1 : low - 1 + count] = sol.astype(jnp.bfloat16)
            if mid:
                spec[element - 2] = part
    rows = slice(window_at + 1, window_at + 1 + inner)
    for pair in (1, 2):
        images = applied(
            packed, 2 * pair, 1, inner, across[pair], (along[2 * pair], along[2 * pair + 1])
        )
        finals = []
        for k, image in enumerate(images):
            element = 2 * pair + k
            final = halves(inverse, element, rows, spec[element - 2, 1 : 1 + inner] - image)
            finals.append(final.astype(jnp.bfloat16).reshape(inner * steps, width))
        delta = jnp.dot(
            backward[...], jnp.concatenate(finals, axis=1), preferred_element_type=jnp.float32
        )
        delta = delta.astype(jnp.bfloat16).astype(jnp.float32)
        for k in range(2):
            element = 2 * pair + k
            part = delta[:, k * width : (k + 1) * width].reshape(inner, steps, width)
            state = values[element + 2, 2 : 2 + inner].astype(jnp.float32) + part
            write(element - 2, state.astype(jnp.bfloat16))


def chooser(core, slots, tiles):
    def weights_of(element):
        row = element - 2 + 4 * core
        if element < 2:
            row = element + 2
        elif element > 5:
            row = element - 2
        places = [0] + [slots[at, row] for at in range(4)] + [5, 6]
        return [tiles[row, place] for place in places]

    return weights_of


def lay_tiles(weights_of, pair, across, along, to_across, to_along):
    width = along.shape[-1]
    for k in range(2):
        own, two_before, before, behind, two_behind, below, above = weights_of(2 * pair + k)
        lanes = slice(k * width, (k + 1) * width)
        for at, block in enumerate((two_before, before, own, behind, two_behind)):
            across[to_across, (at + k) * width : (at + k + 1) * width, lanes] = block
        empty = 5 - 5 * k
        across[to_across, empty * width : (empty + 1) * width, lanes] = jnp.zeros_like(own)
        along[to_along + k, :width] = below
        along[to_along + k, width:] = above


def trim_kernel(count, *rest):
    out = rest[-1]
    for k, piece in enumerate(rest[:count]):
        local, rows, _ = piece.shape
        out[k * local : (k + 1) * local] = piece[:, 4 : rows - 4]


def gather_kernel(places, *rest):
    parts, out = rest[:-1], rest[-1]
    local = parts[0].shape[0]
    mine = lax.axis_index("tm")
    for k, part in zip(places, parts):
        out[pl.ds(lax.bitwise_xor(mine, k) * local, local)] = part[...]


def pack_kernel(start, reaction, source, _, fields):
    for at, field in enumerate((start, reaction, source)):
        fields[at] = field[...]


def first_layer(count, all_layers):
    return chip_rank(lax.axis_index("tm"), count) * (all_layers // count) - APPLICATIONS


def fields_kernel(count, fields, others, diag, slots, _, bundle, edge):
    layers = fields.shape[1]
    core, base = lax.axis_index("layer"), first_layer(count, 2 * layers)
    window = bundle.shape[0] // 3
    for at in range(3):
        for place in range(window):
            layer = jnp.clip(base + place, 0, 2 * layers - 1)
            own = layer // layers == core
            layer = lax.rem(layer, layers)
            row = jnp.where(own, fields[at, layer], others[at, layer])
            bundle[at * window + place] = row
            edge[at * window + place] = jnp.where(core == 0, row[0:2], row[6:8])
    edge[3 * window] = jnp.where(core == 0, diag[0:2], diag[6:8])
    for at in range(2):
        edge[3 * window + 1 + at, :, 0:8] = slots[2 * at : 2 * at + 2].astype(jnp.float32)


def arrive(arrived, order, values, at_elements):
    steps, rows, width = arrived.shape
    size = steps * GROUP * 4
    groups = rows // (GROUP * 4)
    for group in range(0, groups, 2):
        both = [
            arrived[:, place * GROUP * 4 : (place + 1) * GROUP * 4].reshape(size, width)
            for place in range(group, min(group + 2, groups))
        ]
        moved = jnp.dot(
            order[...], jnp.concatenate(both, axis=1), preferred_element_type=jnp.float32
        ).astype(jnp.bfloat16)
        for k in range(len(both)):
            values[pl.ds(at_elements, 4), (group + k) * GROUP : (group + k + 1) * GROUP] = moved[
                :, k * width : (k + 1) * width
            ].reshape(4, GROUP, steps, width)


def edge_tiles_kernel(tiles, out):
    group = lax.axis_index("group")
    count = tiles.shape[1]
    out[:count] = tiles[group]
    out[count:] = tiles[1 - group, : out.shape[0] - count]


def ready_kernel(all_layers, count, slots, order, tiles, bundle, bundle_edge, diag_own, own, beside,
                 coef, diag, inverse, values, across, along, picks):
    core, base = lax.axis_index("layer"), first_layer(count, all_layers)
    arrive(own, order, values, 4)
    arrive(beside, order, values, 8 - 8 * core)
    window = bundle.shape[0] // 3
    width = bundle.shape[2]
    sublane = lax.broadcasted_iota(jnp.int32, (8, width), 0)

    def widened(row, pair):
        turned = jnp.where(core == 0, pltpu.roll(row, 2, 0), pltpu.roll(row, 6, 0))
        for k in range(2):
            turned = jnp.where(
                sublane == 6 * core + k, jnp.broadcast_to(pair[k : k + 1], (8, width)), turned
            )
        return turned

    for at in range(3):
        for place in range(window):
            coef[at, place] = widened(bundle[at * window + place], bundle_edge[at * window + place])
    diag[...] = widened(diag_own[...], bundle_edge[3 * window])
    wide, half = inverse.shape[2:4]
    row = lax.broadcasted_iota(jnp.int32, (half, width), 0)
    eigen = []
    for numbers in transform_tables(2 * half)[2]:
        column = jnp.full((half, width), float(numbers[0]), jnp.float32)
        for at in range(1, half):
            column = jnp.where(row == at, float(numbers[at]), column)
        eigen.append(column)
    layer = lax.broadcasted_iota(jnp.int32, (wide, 1, width), 0) + (base + 1)
    inside = jnp.where((layer >= 0) & (layer < all_layers), 1.0, 0.0).astype(jnp.float32)
    for element in range(8):
        start = coef[0, 1 : 1 + wide, element : element + 1, :]
        reaction = coef[1, 1 : 1 + wide, element : element + 1, :]
        real = diag[element : element + 1, :][None] + 3.0 * reaction * start * start
        near = eigen[0][None] + real
        far = eigen[2][None] + real
        imag = eigen[1][None]
        near_over = inside / (near * near + imag * imag)
        inverse[element, 0] = near * near_over
        inverse[element, 1] = -imag * near_over
        inverse[element, 2] = far * (inside / (far * far + imag * imag))
    weights_of = chooser(core, slots, tiles)
    for pair in range(4):
        lay_tiles(weights_of, pair, across, along, pair, 2 * pair)
    for k in range(2):
        for at in range(4):
            for slot in range(4):
                hit = jnp.where(slots[4 + at, 6 - 6 * core + k] == slot + 1, 1.0, 0.0)
                picks[4 * (4 * k + at) + slot] = jnp.full((8, width), hit, jnp.float32)


def joined(outer, every, each):
    inner = [every.at[k] for k in range(each, 3 * each)]
    outer = [outer.at[k] for k in range(2 * each)]
    return outer[:each] + inner + outer[each:]


def first_kernel(count, sent, order, coef, diag, inverse, ready, near_across, near_along, picks, edge_one,
                 edge_two, forward, backward, early, second, others, out, message, across, along, edge_tiles,
                 arrived, values, packed, spec):
    core, mine, group = lax.axis_index("layer"), lax.axis_index("tm"), lax.axis_index("group")
    rest = 7 - edge_two.shape[0]
    edge_tiles[group] = edge_one[0:7]
    edge_tiles[1 - group, 0:rest] = edge_one[7 : 7 + rest]
    edge_tiles[1 - group, rest:7] = edge_two[...]
    across[1 - core] = near_across[3 - 3 * core]
    along[pl.ds(2 - 2 * core, 2)] = near_along[pl.ds(6 - 6 * core, 2)]

    def weights_of(element):
        blocks = [edge_tiles[element, 0]]
        for at in range(4):
            block = 0.0
            for slot in range(4):
                pick = picks[4 * (4 * element + at) + slot, 0:1].astype(jnp.bfloat16)
                block = block + edge_tiles[element, 1 + slot] * pick
            blocks.append(block)
        return blocks + [edge_tiles[element, 5], edge_tiles[element, 6]]

    lay_tiles(weights_of, 0, across, along, core, 2 * core)
    values[4:8] = ready[4:8]
    values[pl.ds(8 - 8 * core, 4)] = ready[pl.ds(8 - 8 * core, 4)]
    steps, rows, width = arrived.shape
    local = steps // count
    arrived[:, :4] = jnp.zeros((steps, 4, width), jnp.bfloat16)
    arrived[:, rows - 4 :] = jnp.zeros((steps, 4, width), jnp.bfloat16)
    for parts, places in zip((early, second, others), sent):
        for at, k in enumerate(places):
            part = parts[at * local : (at + 1) * local]
            arrived[pl.ds(lax.bitwise_xor(mine, k) * local, local), 4 : rows - 4] = part
    arrive(arrived, order, values, 8 * core)

    def write(element, state):
        out[element] = state

    newton(values, joined(across, near_across, 1), joined(along, near_along, 2), coef, diag, inverse,
           forward, backward, packed, spec, 0, write)
    layers = out.shape[1]
    for at in range(2):
        message[at * (layers - 2) : (at + 1) * (layers - 2)] = out[2 * core + at, 1 : layers - 1]
        begin = 2 * (layers - 2) + at * (layers - 4)
        message[begin : begin + layers - 4] = out[2 - 2 * core + at, 2 : layers - 2]


def second_kernel(count, order, coef, diag, inverse, across, along, near_across, near_along,
                  forward, backward, own, beside, far, out, values, packed, spec, solved):
    core, mine = lax.axis_index("layer"), lax.axis_index("tm")
    layers, steps, width = own.shape[1:]
    values[4:8] = own[...]
    values[pl.ds(8 - 8 * core, 4)] = beside[...]
    for at in range(2):
        values[2 + 6 * core + at, 1 : layers - 1] = far[
            at * (layers - 2) : (at + 1) * (layers - 2)
        ]
        begin = 2 * (layers - 2) + at * (layers - 4)
        values[10 * core + at, 2 : layers - 2] = far[begin : begin + layers - 4]

    def write(element, state):
        solved[element] = state

    newton(values, joined(across, near_across, 1), joined(along, near_along, 2), coef, diag, inverse,
           forward, backward, packed, spec, 2, write)
    size = steps * GROUP * 4
    local = steps // count
    for group in range(solved.shape[1] // GROUP):
        part = solved[:, group * GROUP : (group + 1) * GROUP].reshape(size, width)
        moved = jnp.dot(order[...], part, preferred_element_type=jnp.float32)
        moved = moved.astype(jnp.bfloat16).reshape(steps, GROUP * 4, width)
        cut = pl.ds(group * GROUP * 4, GROUP * 4)
        for goal in range(count):
            side = lax.bitwise_xor(goal % 2, core)
            place = lax.bitwise_xor(goal // 2, mine // 2)
            out[side, pl.ds(place * local, local), cut] = moved[goal * local : (goal + 1) * local]


def last_kernel(count, order, *rest):
    parts, out = rest[:-1], rest[-1]
    steps, layers, elems, width = out.shape
    half = count // 2
    layers //= half
    mine = lax.axis_index("tm")
    for k, part in enumerate(parts):
        both = [part[lax.bitwise_xor(lax.rem(mine, 2), side)].reshape(-1, width) for side in range(2)]
        moved = jnp.dot(
            order[...], jnp.concatenate(both, axis=0), preferred_element_type=jnp.float32
        )
        place = lax.bitwise_xor(mine // 2, k)
        out[:, pl.ds(place * layers, layers)] = moved.reshape(steps, layers, elems, width)


def call(kernel, out_shape, scratch, scalars, arrays, later_than=()):
    vmem = pl.BlockSpec(memory_space=pltpu.VMEM)
    return pl.pallas_call(
        kernel,
        out_shape=out_shape,
        in_specs=[pl.BlockSpec(memory_space=pltpu.SMEM)] * len(scalars)
        + [vmem] * len(arrays)
        + [pl.BlockSpec(memory_space=pl.ANY)] * len(later_than),
        out_specs=jax.tree.map(lambda _: vmem, out_shape),
        scratch_shapes=scratch,
        compiler_params=pltpu.CompilerParams(vmem_limit_bytes=32 * 1024 * 1024),
    )(*scalars, *arrays, *later_than)


def shards(state_guess, start_state, reaction, source, self_diag, tiles, neighbors):
    local_steps, local_layers, local_elems, width = state_guess.shape
    count = lax.axis_size("tm")
    sections = lax.axis_size("space")
    mine, core = lax.axis_index("tm"), lax.axis_index("layer")
    steps = local_steps * count
    all_layers = local_layers * 2
    chip_layers = all_layers // count

    window = -(-(chip_layers + 2 * APPLICATIONS) // GROUP) * GROUP
    half = local_elems // 2
    swap = [(0, 1), (1, 0)]
    circle = []
    for section in range(sections):
        one, other = 2 * section + 1, 2 * ((section + 1) % sections)
        circle += [(one, other), (other, one)]

    def over_core(array):
        return lax.ppermute(array, "layer", swap)

    def over_circle(array):
        return lax.ppermute(array, ("space", "layer"), circle)

    def exchanged(parts):
        return [parts[0]] + [
            lax.ppermute(parts[k], "tm", [(i, i ^ k) for i in range(count)])
            for k in range(1, count)
        ]

    def held(shape, dtype=jnp.bfloat16):
        return jax.ShapeDtypeStruct(shape, dtype)

    pair = state_guess.astype(jnp.bfloat16).reshape(local_steps, local_layers, 2, half, width)
    flat = (local_steps, local_layers * half, width)
    keep = lax.dynamic_index_in_dim(pair, core, 2, keepdims=False).reshape(flat)
    give = lax.dynamic_index_in_dim(pair, 1 - core, 2, keepdims=False).reshape(flat)
    got = over_core(give)
    below = jnp.zeros((local_steps, APPLICATIONS * half, width), jnp.bfloat16)
    above = jnp.zeros(
        (local_steps, (window - chip_layers - APPLICATIONS) * half, width), jnp.bfloat16
    )
    whole = jnp.concatenate(
        [below, jnp.where(core == 0, keep, got), jnp.where(core == 0, got, keep), above], 1
    )
    pieces = [
        lax.dynamic_slice_in_dim(
            whole, chip_rank(lax.bitwise_xor(mine, k), count) * (chip_layers * half), window * half, 1
        )
        for k in range(count)
    ]
    chunks = exchanged(pieces)
    rest = tiles.shape[1] - OVER_GROUP
    edge_one = call(
        edge_tiles_kernel,
        held((tiles.shape[1] + rest,) + tiles.shape[2:]),
        [],
        [],
        [lax.dynamic_slice_in_dim(tiles, 6 * core, 2, 0)],
    )
    edge_one = over_circle(edge_one)
    edge_two = lax.ppermute(edge_one[rest : tiles.shape[1]], "group", swap)
    turn = sorted(range(1, count), key=lambda k: (k < count // 2, -k))

    def trimmed(parts, later_than):
        return call(
            lambda *refs: trim_kernel(len(parts), *refs),
            held((local_steps * len(parts), (window - 2) * half, width)),
            [],
            [],
            [chunks[k] for k in parts],
            later_than,
        )

    sent = [[0], turn[:1], turn[1:]]
    across = [over_circle(trimmed(sent[0], [])), over_circle(trimmed(sent[1], []))]
    across.append(over_circle(trimmed(sent[2], [across[0], edge_one])))

    places = [0] + turn
    own = call(
        lambda *refs: gather_kernel(places, *refs),
        held((steps, window * half, width)),
        [],
        [],
        [chunks[k] for k in places],
    )

    fields = call(
        pack_kernel,
        held((3,) + start_state.shape, jnp.float32),
        [],
        [],
        [start_state, reaction, source],
        [pieces[1]],
    )
    total = local_elems * sections
    number = local_elems * lax.axis_index("space") + jnp.arange(local_elems, dtype=jnp.int32)
    wanted = (number[None] + jnp.array(OFFSETS, jnp.int32)[:, None] + total) % total
    ids = neighbors.T
    slots = 1 + sum(at * (ids[at : at + 1] == wanted).astype(jnp.int32) for at in range(1, 4))
    bundle, bundle_edge = call(
        lambda *refs: fields_kernel(count, *refs),
        (
            held((3 * window, local_elems, width), jnp.float32),
            held((3 * window + 3, 2, width), jnp.float32),
        ),
        [],
        [],
        [fields, over_core(fields), self_diag, slots],
        [chunks[turn[0]]],
    )
    bundle_edge = over_circle(bundle_edge)
    edge_slots = bundle_edge[3 * window + 1 :, :, :local_elems].reshape(4, local_elems)
    slots = jnp.concatenate([slots, edge_slots.astype(jnp.int32)], 0)

    forward, backward, _ = transform_tables(steps)
    order = np.zeros((4, GROUP, steps, steps, GROUP, 4), np.float32)
    for element in range(4):
        for layer in range(GROUP):
            order[element, layer, :, :, layer, element] = np.eye(steps)
    order = order.reshape(4 * GROUP * steps, steps * GROUP * 4)
    last = window - 8
    order_last = np.zeros(
        (local_steps, chip_layers, 2, half, 2, local_steps, last, half), np.float32
    )
    for step in range(local_steps):
        for layer in range(chip_layers):
            for side in range(2):
                order_last[step, layer, side, :, side, step, layer, :] = np.eye(half)
    order_last = order_last.reshape(local_steps * chip_layers * 2 * half, -1)

    def constant(matrix):
        return jnp.asarray(matrix.astype(jnp.bfloat16))

    def table(matrix, layers):
        return constant(np.kron(np.eye(layers), matrix))

    def scratch(layers):
        return [
            pltpu.VMEM((12, layers, steps, width), jnp.bfloat16),
            pltpu.VMEM((8, layers - 2, steps, width), jnp.bfloat16),
            pltpu.VMEM((4, layers - 2, steps, width), jnp.float32),
        ]

    total = local_elems * sections
    arrived = pltpu.VMEM((steps, window * half, width), jnp.bfloat16)
    laid = (held((4, 6 * width, 2 * width)), held((8, 2 * width, width)))
    coef, diag, inverse, ready, near_across, near_along, picks = call(
        lambda *refs: ready_kernel(all_layers, count, *refs),
        (
            held((3, window, 8, width), jnp.float32),
            held((8, width), jnp.float32),
            held((8, 3, window - 2, steps // 2, width), jnp.float32),
            held((12, window, steps, width)),
            *laid,
            held((32, 8, width), jnp.float32),
        ),
        [],
        [slots],
        [constant(order), tiles, bundle, bundle_edge, self_diag, own, over_core(own)],
    )
    state, edge, *outer = call(
        lambda *refs: first_kernel(count, sent, *refs),
        (
            held((4, window - 4, steps, width)),
            held((2 * (window - 6) + 2 * (window - 8), steps, width)),
            held((2, 6 * width, 2 * width)),
            held((4, 2 * width, width)),
        ),
        [pltpu.VMEM((2,) + tiles.shape[1:], jnp.bfloat16), arrived] + scratch(window),
        [],
        [constant(order), coef, diag, inverse, ready, near_across, near_along, picks, edge_one,
         edge_two, table(forward, window - 2), table(backward, window - 4), *across],
    )
    solved = call(
        lambda *refs: second_kernel(count, *refs),
        held((2, steps // 2, last * half, width)),
        scratch(window - 4) + [pltpu.VMEM((4, last, steps, width), jnp.bfloat16)],
        [],
        [constant(order.T), coef, diag, inverse, *outer, near_across, near_along,
         table(forward, window - 6), table(backward, last),
         state, over_core(state), over_circle(edge)],
    )

    keep, got = solved[0], over_core(solved[1])
    parts = []
    for k in range(count // 2):
        cut = slice(k * local_steps, (k + 1) * local_steps)
        pairs = []
        for device in range(count):
            for side in range(2):
                goal = 2 * (device // 2 ^ k) + side
                pairs.append((2 * device + side, 2 * goal + device % 2))
        parts.append(lax.ppermute(jnp.stack([keep[cut], got[cut]]), ("tm", "layer"), pairs))
    return call(
        lambda *refs: last_kernel(count, *refs),
        held(state_guess.shape, jnp.float32),
        [],
        [],
        [constant(order_last), *parts],
    )


def solution(mesh):
    in_specs = (
        P("tm", ("group", "layer"), "space", None),
        P(("group", "layer"), "space", None),
        P(("group", "layer"), "space", None),
        P(("group", "layer"), "space", None),
        P("space", None),
        P("space", None, None, None),
        P("space", None),
    )
    out_specs = P("tm", ("group", "layer"), "space", None)
    return jax.shard_map(shards, mesh=mesh, in_specs=in_specs, out_specs=out_specs, check_vma=False)
```
